32 devices in a mesh: patch: 32 (over z, y, x, core).
Axes of the slice: x: 2, y: 2, z: 4, core: 2. Of those that a mesh axis runs over, the one named last changes fastest.
Arguments:
- inputs: bfloat16 [96, 32, 32, 128], P('patch'), may hold values from -6 to 6
- cotangent: bfloat16 [96, 32, 32, 128], P('patch'), may hold values from -6 to 6
- weights: bfloat16 [3, 3, 128, 128], replicated, may hold values from -0.1875 to 0.1875
- bias_vector: float32 [128], replicated, may hold values from -3 to 3
- neighbours: int32 [96, 8], P('patch'), may hold values from 0 to 95, as said below
- rotations: int32 [96, 8], P('patch'), may hold values from 0 to 3
- corners: int32 [96, 8], P('patch'), may hold values from 0 to 1, as said below
Outputs:
- outputs: bfloat16 [96, 32, 32, 128], P('patch')
- input_grad: bfloat16 [96, 32, 32, 128], P('patch')
- weight_grad: float32 [3, 3, 128, 128], replicated
- bias_grad: float32 [128], replicated
The draws below stay inside these ranges and needn't reach their ends.
Inputs may be any that keep to these rules, and one draw needn't show every extreme that they name: `neighbours`: the neighbour of a patch on device d lies on a device d + o (modulo the device count) with |o| <= 2; offsets 2 and -2 both occur. `corners`: the four side directions are always 1.
All inputs are finite; a program needn't handle non-finite values.
Results may differ from the reference program's by a relative error of at most 0.0035.
Values may be sent and summed in bfloat16 or wider, within the bound.
No kernel may reach another device: no remote copies, remote signals or barrier semaphores. Data moves between devices by JAX's collectives and lax.ppermute only.
A program may use at most 64 MiB of HBM per device.

```python
import math
import jax
import jax.numpy as jnp
from jax import lax

CH = 128
SIDE = 32
REACH = 2
PATCH_DEV = 3
PATCHES = 96


def draw_neighbours(key, part):
    key_off = jax.random.fold_in(key, 11)
    key_pos = jax.random.fold_in(key, 12)
    devices_all = PATCHES // PATCH_DEV
    rows = jnp.arange(PATCHES)
    owners = rows // PATCH_DEV
    offset = jax.random.randint(key_off, (PATCHES, 8), -REACH, REACH + 1)
    offset = offset.at[0, 1].set(REACH).at[0, 6].set(-REACH)
    offset = offset.at[0, 0].set(-1).at[PATCH_DEV, 3].set(-1)
    within = jax.random.randint(key_pos, (PATCHES, 8), 0, PATCH_DEV)
    within = within.at[0, 0].set(PATCH_DEV - 1).at[PATCH_DEV, 3].set(0)
    target = (owners[:, None] + offset) % devices_all
    return (target * PATCH_DEV + within).astype(jnp.int32)


def draw_corners(key, part):
    key_flag = jax.random.fold_in(key, 21)
    values = jax.random.randint(key_flag, (PATCHES, 8), 0, 4)
    diagonal = jnp.array([1, 0, 1, 0, 0, 1, 0, 1], dtype=jnp.int32)[None, :]
    flags = jnp.where(values > 0, 1, 0)
    flags = jnp.where(diagonal > 0, flags, 1)
    flags = flags.at[0, 0].set(0).at[0, 2].set(1)
    return flags.astype(jnp.int32)


def set_ends(values, own_key, least, largest):
    extent = values.shape
    place = [jax.random.randint(jax.random.fold_in(own_key, axis), (), 0, extent[axis]) for axis in range(len(extent))]
    values = values.at[tuple(place)].set(least)
    longest = extent.index(max(extent))
    place[longest] = (place[longest] + 1) % extent[longest]
    return values.at[tuple(place)].set(largest)


def block_scale(stream_key, extent, cuts, low, largest):
    level, own = 1.0, jax.random.fold_in(stream_key, 6)
    for dim, blocks in cuts:
        steps = jnp.exp(jax.random.uniform(jax.random.fold_in(own, dim), (blocks,), jnp.float32, low / len(cuts), largest / len(cuts)))
        level = level * jnp.repeat(steps, extent[dim] // blocks).reshape([-1 if axis == dim else 1 for axis in range(len(extent))])
    return level


def bell_draw(key, dims, spread, most, cuts=(), kind=jnp.bfloat16):
    drawn = spread * jax.random.normal(key, dims, jnp.float32)
    if cuts:
        drawn = drawn * block_scale(key, dims, cuts, -0.22, 0.18)
    return jnp.clip(drawn, -most, most).astype(kind)


def setup_inputs(seed: int = 0) -> dict:
    streams_of = jax.random.split(jax.random.key(seed), 8)
    inputs = bell_draw(streams_of[0], (PATCHES, SIDE, SIDE, CH), 1.0, 6.0, ((0, 32),))
    cotangent = bell_draw(streams_of[1], (PATCHES, SIDE, SIDE, CH), 1.0, 6.0, ((0, 32),))
    weights = bell_draw(streams_of[2], (3, 3, CH, CH), (9 * CH) ** -0.5, 0.1875)
    bias_vector = bell_draw(streams_of[3], (CH,), 0.5, 3.0, (), jnp.float32)
    neighbours = draw_neighbours(jax.random.fold_in(streams_of[7], 71), 0)
    rotations = set_ends(jax.random.randint(streams_of[5], (PATCHES, 8), 0, 4), jax.random.fold_in(streams_of[5], 1), 0, 3).astype(jnp.int32)
    corners = draw_corners(jax.random.fold_in(streams_of[7], 71), 0)
    return dict(inputs=inputs, cotangent=cotangent, weights=weights, bias_vector=bias_vector, neighbours=neighbours, rotations=rotations, corners=corners)


DIRECTIONS = ((-1, -1), (-1, 0), (-1, 1), (0, -1), (0, 1), (1, -1), (1, 0), (1, 1))

def aligned_span(step, length):
    if step < 0:
        return slice(length - 2, length)
    if step == 0:
        return slice(0, length)
    return slice(0, 2)

def edge_strips(patches):
    length = patches.shape[1]
    upper = patches[:, 0:2]
    lower = patches[:, length - 2:]
    rows = jnp.arange(length)
    inside = ((rows >= 2) & (rows < length - 2))[None, None, :, None]
    left_cols = jnp.swapaxes(patches[:, :, 0:2], 1, 2)
    left_cols = jnp.where(inside, left_cols, jnp.zeros_like(left_cols))
    right_cols = jnp.swapaxes(patches[:, :, length - 2:], 1, 2)
    right_cols = jnp.where(inside, right_cols, jnp.zeros_like(right_cols))
    return jnp.stack([upper, lower, left_cols, right_cols], axis=1)

def edge_frame(strips):
    length = strips.shape[3]
    upper = strips[:, 0]
    lower = strips[:, 1]
    left_cols = jnp.swapaxes(strips[:, 2], 1, 2)[:, 2:length - 2]
    right_cols = jnp.swapaxes(strips[:, 3], 1, 2)[:, 2:length - 2]
    hollow = jnp.zeros((strips.shape[0], length - 4, length - 4, strips.shape[4]), strips.dtype)
    middle = jnp.concatenate([left_cols, hollow, right_cols], axis=2)
    return jnp.concatenate([upper, middle, lower], axis=1)

def rotate_frame(frames, quarter):
    turns = quarter[:, None, None, None]
    result = jnp.where(turns == 0, frames, jnp.zeros_like(frames))
    for k in range(1, 4):
        result = jnp.where(turns == k, jnp.rot90(frames, k, axes=(1, 2)), result)
    return result

def extend_patch(center, gathered, rotations, corners):
    pieces = {}
    for j, (row_step, col_step) in enumerate(DIRECTIONS):
        length = center.shape[1]
        aligned = rotate_frame(edge_frame(gathered[:, j]), rotations[:, j])
        region = aligned[:, aligned_span(row_step, length), aligned_span(col_step, length)]
        present = corners[:, j][:, None, None, None] > 0
        pieces[row_step, col_step] = jnp.where(present, region, jnp.zeros_like(region))
    upper = jnp.concatenate([pieces[-1, -1], pieces[-1, 0], pieces[-1, 1]], axis=2)
    middle = jnp.concatenate([pieces[0, -1], center, pieces[0, 1]], axis=2)
    lower = jnp.concatenate([pieces[1, -1], pieces[1, 0], pieces[1, 1]], axis=2)
    return jnp.concatenate([upper, middle, lower], axis=1)

def dilated_conv(extended, kernel):
    return lax.conv_general_dilated(extended, kernel, (1, 1), 'VALID', rhs_dilation=(2, 2), dimension_numbers=('NHWC', 'HWIO', 'NHWC'), precision=lax.Precision.HIGHEST, preferred_element_type=jnp.float32)

def reference(inputs, cotangent, weights, bias_vector, neighbours, rotations, corners):
    inputs_wide = inputs.astype(jnp.float32)
    weight_wide = weights.astype(jnp.float32)
    groups = jnp.arange(PATCHES).astype(jnp.int32).reshape(-1, PATCH_DEV)

    def forward(source, kernel, offsets):
        strips_all = edge_strips(source)

        def single(members):
            gathered = strips_all[neighbours[members]]
            extended = extend_patch(source[members], gathered, rotations[members], corners[members])
            return dilated_conv(extended, kernel) + offsets
        result = lax.map(jax.checkpoint(single), groups)
        return result.reshape(PATCHES, SIDE, SIDE, CH)
    result, pullback = jax.vjp(forward, inputs_wide, weight_wide, bias_vector)
    grad_in, grad_weight, grad_bias = pullback(cotangent.astype(jnp.float32))
    factor = 1.0 / (SIDE * math.sqrt(PATCHES))
    return (result.astype(jnp.bfloat16), grad_in.astype(jnp.bfloat16), grad_weight * factor, grad_bias * factor)
```

```python
import functools
import math

import jax
import jax.numpy as jnp
import numpy as np
from jax import lax
from jax.experimental import pallas as pl
from jax.experimental.pallas import tpu as pltpu
from jax.sharding import PartitionSpec as P

REACH = 2
BF = jnp.bfloat16
F32 = jnp.float32

DIRECTIONS = ((-1, -1), (-1, 0), (-1, 1), (0, -1), (0, 1), (1, -1), (1, 0), (1, 1))
SIDE_TABLE = (
    ((0, 0), (3, 1), (1, 3), (2, 2)),
    ((1, 0), (2, 1), (0, 3), (3, 2)),
    ((2, 0), (0, 2), (3, 3), (1, 1)),
    ((3, 0), (1, 2), (2, 3), (0, 1)),
)
SIDE_DIRECTION = (1, 6, 3, 4)
SIDE_ENDS = ((0, 2), (5, 7))
SIDE_TAPS = (((0, 0), (0, 1), (0, 2)), ((2, 0), (2, 1), (2, 2)), ((0, 0), (1, 0), (2, 0)), ((0, 2), (1, 2), (2, 2)))


def wanted_side(row_step, col_step):
    if row_step < 0:
        return 1
    if row_step > 0:
        return 0
    return 3 if col_step < 0 else 2


def flip_tables(length):
    size = 2 * length
    flips = np.zeros((4, size, size), np.float32)
    for code in range(4):
        for r in range(2):
            for k in range(length):
                rr = 1 - r if code & 1 else r
                kk = length - 1 - k if code & 2 else k
                flips[code, r * length + k, rr * length + kk] = 1
    back = np.zeros((2, size, size), np.float32)
    ahead = np.zeros((2, size, size), np.float32)
    for r in range(2):
        for k in range(length):
            back[int(k < 2), r * length + k, r * length + (k - 2) % length] = 1
            ahead[int(k >= length - 2), r * length + k, r * length + (k + 2) % length] = 1
    sides = np.stack([np.concatenate([back[0] @ f, f, ahead[0] @ f]) for f in flips])
    ends = np.stack([np.concatenate([back[1] @ f, ahead[1] @ f]) for f in flips])
    return flips, sides, ends


def place_of(me, neighbour, rotation, which, patches_here, devices):
    owner = lax.div(neighbour, patches_here)
    within = neighbour - owner * patches_here
    offset = owner - me
    offset = jnp.where(offset < 0, offset + devices, offset)
    core = lax.rem(me, 2)
    to_mate = jnp.where(core == 0, 1, devices - 1)
    block = jnp.where(offset == to_mate, 3, 4)
    block = jnp.where(offset == 2, 2, block)
    block = jnp.where(offset == devices - 2, 1, block)
    block = jnp.where(offset == 0, 0, block)
    slot, code = SIDE_TABLE[which][0]
    for k in range(1, 4):
        slot = jnp.where(rotation == k, SIDE_TABLE[which][k][0], slot)
        code = jnp.where(rotation == k, SIDE_TABLE[which][k][1], code)
    return (block * patches_here + within) * 4 + slot, code


def dot(a, b):
    return jnp.dot(a, b, preferred_element_type=F32)


def column_strip(wide_ref, first, length):
    return jnp.concatenate([wide_ref[pl.ds(first + c, length, stride=length), :] for c in range(2)], axis=0)


def add_columns(wide_ref, first, length, strip):
    for c in range(2):
        at = pl.ds(first + c, length, stride=length)
        wide_ref[at, :] = wide_ref[at, :] + strip[c * length : (c + 1) * length]


def spread(ext_ref, wide, length):
    count = length * length
    column = lax.broadcasted_iota(jnp.int32, (count, 1), 0) & (length - 1)
    pad = 2 * length
    back = jnp.where(column >= 2, pltpu.roll(wide, 2, 0), 0.0)
    ahead = jnp.where(column < length - 2, pltpu.roll(wide, count - 2, 0), 0.0)
    ext_ref[pad : pad + count, 0:128] = back.astype(BF)
    ext_ref[pad : pad + count, 128:256] = wide.astype(BF)
    ext_ref[pad : pad + count, 256:384] = ahead.astype(BF)


def clear_rows(ext_ref, length):
    pad = 2 * length
    empty = jnp.zeros((pad, 384), BF)
    ext_ref[0:pad, :] = empty
    ext_ref[pad + length * length :, :] = empty


def pack_kernel(x_ref, out_ref, wide_ref, *, length):
    count = length * length
    for p in range(x_ref.shape[0]):
        out_ref[4 * p] = x_ref[p, 0 : 2 * length, :]
        out_ref[4 * p + 1] = x_ref[p, count - 2 * length :, :]
        wide_ref[...] = x_ref[p].astype(F32)
        out_ref[4 * p + 2] = column_strip(wide_ref, 0, length).astype(BF)
        out_ref[4 * p + 3] = column_strip(wide_ref, length - 2, length).astype(BF)


def local_kernel(
    me_ref, nb_ref, rot_ref, cor_ref, x_ref, cot_ref, w_ref, flip_ref,
    dw_ref, bias_ref, dx_ref, strips_ref, own_ref, far_ref, near_ref,
    ext_ref, wide_ref, pool_ref, *, length, devices,
):
    patches = x_ref.shape[0]
    count = length * length
    me = me_ref[0]
    clear_rows(ext_ref, length)
    pool_ref[...] = jnp.zeros_like(pool_ref)
    total_bias = jnp.zeros((1, 128), F32)
    chunk = min(count, 256)
    flipped = [
        jnp.concatenate([w_ref[(2 - a) * 3 + 2], w_ref[(2 - a) * 3 + 1], w_ref[(2 - a) * 3]], axis=1) for a in range(3)
    ]
    along = lax.broadcasted_iota(jnp.int32, (length, 1), 0)
    for p in range(patches):
        wide = cot_ref[p].astype(F32)
        wide_ref[...] = wide
        total_bias = total_bias + jnp.sum(wide, axis=0, keepdims=True)
        spread(ext_ref, wide, length)
        strips = [
            cot_ref[p, 0 : 2 * length, :],
            cot_ref[p, count - 2 * length :, :],
            column_strip(wide_ref, 0, length).astype(BF),
            column_strip(wide_ref, length - 2, length).astype(BF),
        ]
        for s in range(4):
            strips_ref[s, 2 * length * p : 2 * length * (p + 1), :] = strips[s]
            taps = [w_ref[a * 3 + b] for a, b in SIDE_TAPS[s]]
            terms = lax.dot_general(
                strips[s], jnp.concatenate(taps, axis=0), (((1,), (1,)), ((), ())), preferred_element_type=F32
            )
            side, first, last = [], [], []
            for r in range(2):
                rows = slice(r * length, (r + 1) * length)
                ahead = pltpu.roll(terms[rows, 0:128], length - 2, 0)
                back = pltpu.roll(terms[rows, 256:384], 2, 0)
                side.append(
                    terms[rows, 128:256]
                    + jnp.where(along < length - 2, ahead, 0.0)
                    + jnp.where(along >= 2, back, 0.0)
                )
                first.append(jnp.where(along >= length - 2, ahead, 0.0))
                last.append(jnp.where(along < 2, back, 0.0))
            sent = [(SIDE_DIRECTION[s], side)]
            if s < 2:
                sent += [(SIDE_ENDS[s][0], first), (SIDE_ENDS[s][1], last)]
            for j, term in sent:
                where_to, code = place_of(
                    me, nb_ref[p, j], rot_ref[p, j], wanted_side(*DIRECTIONS[j]), patches, devices
                )
                value = dot(flip_ref[code], jnp.concatenate(term, axis=0).astype(BF))
                value = value * (cor_ref[p, j] > 0).astype(F32)
                pool_ref[where_to] = pool_ref[where_to] + value
        turned = x_ref[p].T
        for a in range(3):
            grads = dot(turned, ext_ref[2 * length * a : 2 * length * a + count, :])
            for b in range(3):
                tap = (2 - a) * 3 + 2 - b
                rows = slice(tap * 128, (tap + 1) * 128)
                part = grads[:, b * 128 : (b + 1) * 128]
                dw_ref[rows, :] = part if p == 0 else dw_ref[rows, :] + part
        for start in range(0, count, chunk):
            total = None
            for a in range(3):
                at = start + 2 * length * a
                part = lax.dot_general(
                    ext_ref[at : at + chunk, :], flipped[a], (((1,), (1,)), ((), ())), preferred_element_type=F32
                )
                total = part if total is None else total + part
            dx_ref[p, start : start + chunk, :] = total.astype(BF)
    bias_ref[...] = jnp.broadcast_to(total_bias, bias_ref.shape)
    block = 4 * patches
    own_ref[...] = pool_ref[0:block]
    far_ref[...] = pool_ref[block : 3 * block]
    near_ref[...] = pool_ref[3 * block :].astype(BF)


def halo_kernel(
    me_ref, nb_ref, rot_ref, cor_ref, own_ref, low_ref, high_ref, mate_ref, across_ref, strips_ref, dw_ref, bias_ref,
    side_ref, end_ref, out_ref, halo_ref, pool_ref, *, length, devices, factor,
):
    block = own_ref.shape[0]
    patches = block // 4
    for i, source in enumerate((own_ref, low_ref, high_ref, mate_ref, across_ref)):
        pool_ref[i * block : (i + 1) * block] = source[...]
    me = me_ref[0]
    size = 2 * length
    for p in range(patches):

        def fetch(j):
            at, code = place_of(me, nb_ref[p, j], rot_ref[p, j], wanted_side(*DIRECTIONS[j]), patches, devices)
            return pool_ref[at], code

        for s in range(4):
            source, code = fetch(SIDE_DIRECTION[s])
            shifted = dot(side_ref[code], source)
            parts = [shifted[0:size], shifted[size : 2 * size], shifted[2 * size :]]
            if s < 2:
                for which, j in ((0, SIDE_ENDS[s][0]), (1, SIDE_ENDS[s][1])):
                    source, code = fetch(j)
                    corner = dot(end_ref[code, which * size : (which + 1) * size, :], source)
                    parts[2 * which] = parts[2 * which] + corner * (cor_ref[p, j] > 0).astype(F32)
            for i in range(3):
                halo_ref[s, p * size : (p + 1) * size, i * 128 : (i + 1) * 128] = parts[i].astype(BF)
    out_ref[0 : 9 * 128, :] = dw_ref[...]
    for s in range(4):
        grads = lax.dot_general(
            halo_ref[s], strips_ref[s], (((0,), (0,)), ((), ())), preferred_element_type=F32
        )
        for i, (a, b) in enumerate(SIDE_TAPS[s]):
            rows = slice((a * 3 + b) * 128, (a * 3 + b + 1) * 128)
            out_ref[rows, :] = out_ref[rows, :] + grads[i * 128 : (i + 1) * 128]
    out_ref[0 : 9 * 128, :] = out_ref[0 : 9 * 128, :] * factor
    out_ref[9 * 128 : 9 * 128 + 8, :] = bias_ref[...] * factor
    out_ref[9 * 128 + 8 :, :] = jnp.zeros((out_ref.shape[0] - 9 * 128 - 8, 128), F32)


def forward_kernel(x_ref, w_ref, bias_ref, halo_ref, out_ref, ext_ref, wide_ref, *, length):
    patches = x_ref.shape[0]
    count = length * length
    size = 2 * length
    chunk = min(count, 256)
    clear_rows(ext_ref, length)
    borders = []
    for s in range(4):
        taps = jnp.concatenate([w_ref[a * 3 + b] for a, b in SIDE_TAPS[s]], axis=0)
        borders.append(dot(halo_ref[s], taps))
    rows_of = [jnp.concatenate([w_ref[a * 3 + b] for b in range(3)], axis=0) for a in range(3)]
    for p in range(patches):
        spread(ext_ref, x_ref[p].astype(F32), length)
        for start in range(0, count, chunk):
            total = jnp.broadcast_to(bias_ref[...], (chunk, 128))
            for a in range(3):
                at = start + size * a
                total = total + dot(ext_ref[at : at + chunk, :], rows_of[a])
            wide_ref[start : start + chunk, :] = total
        mine = slice(p * size, (p + 1) * size)
        wide_ref[0:size, :] = wide_ref[0:size, :] + borders[0][mine]
        wide_ref[count - size :, :] = wide_ref[count - size :, :] + borders[1][mine]
        add_columns(wide_ref, 0, length, borders[2][mine])
        add_columns(wide_ref, length - 2, length, borders[3][mine])
        out_ref[p] = wide_ref[...].astype(BF)


def join_kernel(dx_ref, own_ref, mate_ref, low_ref, high_ref, out_ref, wide_ref, *, length):
    count = length * length
    size = 2 * length
    for p in range(dx_ref.shape[0]):
        wide_ref[...] = dx_ref[p].astype(F32)
        strips = []
        for s in range(4):
            i = 4 * p + s
            strips.append(
                own_ref[i] + mate_ref[i].astype(F32) + low_ref[i].astype(F32) + high_ref[i].astype(F32)
            )
        wide_ref[0:size, :] = wide_ref[0:size, :] + strips[0]
        wide_ref[count - size :, :] = wide_ref[count - size :, :] + strips[1]
        add_columns(wide_ref, 0, length, strips[2])
        add_columns(wide_ref, length - 2, length, strips[3])
        out_ref[p] = wide_ref[...].astype(BF)


def vmem():
    return pl.BlockSpec(memory_space=pltpu.VMEM)


def smem():
    return pl.BlockSpec(memory_space=pltpu.SMEM)


def call(kernel, name, n_smem, n_vmem, outs, scratch, flops, nbytes):
    return pl.pallas_call(
        kernel,
        name=name,
        out_shape=outs,
        in_specs=[smem()] * n_smem + [vmem()] * n_vmem,
        out_specs=jax.tree.map(lambda _: vmem(), outs),
        scratch_shapes=scratch,
        compiler_params=pltpu.CompilerParams(vmem_limit_bytes=40 * 1024 * 1024),
        cost_estimate=pl.CostEstimate(flops=flops, bytes_accessed=nbytes, transcendentals=0),
    )


def shifted(value, steps):
    count = lax.axis_size("patch")
    return lax.ppermute(value, "patch", [(d, (d + steps) % count) for d in range(count)])


def swapped(value, mask):
    return lax.ppermute(value, "patch", [(d, d ^ mask) for d in range(lax.axis_size("patch"))])


def part_of(value, index, size):
    return lax.dynamic_slice_in_dim(value, index * size, size)


def summed(value, me, devices):
    rows = value.shape[0]
    core = me % 2
    half = rows // 2
    mine = part_of(value, core, half) + swapped(part_of(value, 1 - core, half), 1)
    quarter = half // 4
    at = (me // 2) % 4
    arrived = [swapped(part_of(mine, at ^ k, quarter).astype(BF), 2 * k) for k in range(1, 4)]
    mine = part_of(mine, at, quarter)
    for a in arrived:
        mine = mine + a.astype(F32)
    step = 8
    while step < devices:
        sent = mine.astype(BF)
        mine = sent.astype(F32) + swapped(sent, step).astype(F32)
        if 2 * step < devices:
            other = swapped(sent, 2 * step).astype(F32) + swapped(sent, 3 * step).astype(F32)
            mine = mine + other
        step *= 4
    pieces = jnp.stack([mine] + [swapped(mine, 2 * k) for k in range(1, 4)])
    whole = jnp.concatenate([lax.dynamic_index_in_dim(pieces, at ^ k, 0, False) for k in range(4)])
    other = swapped(whole, 1)
    low = jnp.where(core == 0, whole, other)
    high = jnp.where(core == 0, other, whole)
    return jnp.concatenate([low, high])


def body(inputs, cotangent, weights, bias_vector, neighbours, rotations, corners):
    patches, length, _, chans = inputs.shape
    devices = lax.axis_size("patch")
    count = length * length
    size = 2 * length
    block = 4 * patches
    me = lax.axis_index("patch")
    me_arr = me.reshape(1).astype(jnp.int32)
    core = me % 2
    x = inputs.reshape(patches, count, chans)
    cot = cotangent.reshape(patches, count, chans)
    w = weights.reshape(9, chans, chans)
    flips, sides, ends = (jnp.asarray(t, BF) for t in flip_tables(length))
    strip_block = jax.ShapeDtypeStruct((block, size, chans), BF)
    strip_block_wide = jax.ShapeDtypeStruct((block, size, chans), F32)
    conv_flops = 2 * 9 * patches * count * chans * chans

    edges = call(
        functools.partial(pack_kernel, length=length), "pack_edges", 0, 1, strip_block,
        [pltpu.VMEM((count, chans), F32)], 0, 2 * x.size,
    )(x)
    from_low = shifted(edges, 2)
    from_high = shifted(edges, -2)
    from_mate = swapped(edges, 1)
    from_across = swapped(jnp.where(core == 0, from_high, from_low), 1)

    dw, bias_part, dx, strips, own, far, near = call(
        functools.partial(local_kernel, length=length, devices=devices), "own_pixels", 4, 4,
        (
            jax.ShapeDtypeStruct((9 * chans, chans), F32),
            jax.ShapeDtypeStruct((8, chans), F32),
            jax.ShapeDtypeStruct((patches, count, chans), BF),
            jax.ShapeDtypeStruct((4, patches * size, chans), BF),
            strip_block_wide,
            jax.ShapeDtypeStruct((2 * block, size, chans), F32),
            jax.ShapeDtypeStruct((2 * block, size, chans), BF),
        ),
        [
            pltpu.VMEM((count + 2 * size, 3 * chans), BF),
            pltpu.VMEM((count, chans), F32),
            pltpu.VMEM((5 * block, size, chans), F32),
        ],
        2 * conv_flops, 6 * x.size,
    )(me_arr, neighbours, rotations, corners, x, cot, w, flips)

    factor = 1.0 / (length * math.sqrt(patches * devices))
    grads, halo = call(
        functools.partial(halo_kernel, length=length, devices=devices, factor=factor), "halo_kernel_grad", 4, 10,
        (
            jax.ShapeDtypeStruct((10 * chans, chans), F32),
            jax.ShapeDtypeStruct((4, patches * size, 3 * chans), BF),
        ),
        [pltpu.VMEM((5 * block, size, chans), BF)],
        conv_flops // 8, 2 * x.size,
    )(me_arr, neighbours, rotations, corners, edges, from_low, from_high, from_mate, from_across, strips, dw,
      bias_part, sides, ends)

    total = summed(grads, me, devices)

    outputs = call(
        functools.partial(forward_kernel, length=length), "forward", 0, 4,
        jax.ShapeDtypeStruct((patches, count, chans), BF),
        [pltpu.VMEM((count + 2 * size, 3 * chans), BF), pltpu.VMEM((count, chans), F32)],
        conv_flops, 4 * x.size,
    )(x, w, bias_vector.reshape(1, chans), halo)

    near_in = swapped(near, 1)
    mate_terms, cross_terms = near_in[:block], near_in[block:].astype(F32)
    to_low = (far[:block] + jnp.where(core == 1, cross_terms, 0.0)).astype(BF)
    to_high = (far[block:] + jnp.where(core == 0, cross_terms, 0.0)).astype(BF)
    terms_high = shifted(to_low, -2)
    terms_low = shifted(to_high, 2)
    input_grad = call(
        functools.partial(join_kernel, length=length), "join_input_grad", 0, 5,
        jax.ShapeDtypeStruct((patches, count, chans), BF),
        [pltpu.VMEM((count, chans), F32)], 0, 5 * x.size,
    )(dx, own, mate_terms, terms_low, terms_high)

    weight_grad = total[: 9 * chans].reshape(weights.shape)
    bias_grad = total[9 * chans]
    return (outputs.reshape(inputs.shape), input_grad.reshape(inputs.shape), weight_grad, bias_grad)


def solution(mesh):
    in_specs = (
        P("patch", None, None, None),
        P("patch", None, None, None),
        P(),
        P(),
        P("patch", None),
        P("patch", None),
        P("patch", None),
    )
    out_specs = (P("patch", None, None, None), P("patch", None, None, None), P(), P())
    return jax.shard_map(body, mesh=mesh, in_specs=in_specs, out_specs=out_specs, check_vma=False)
```

```python
import functools
import math

import jax
import jax.numpy as jnp
import numpy as np
from jax import lax
from jax.experimental import pallas as pl
from jax.experimental.pallas import tpu as pltpu
from jax.sharding import PartitionSpec as P

ROOM = 12
BF = jnp.bfloat16
F32 = jnp.float32

DIRECTIONS = ((-1, -1), (-1, 0), (-1, 1), (0, -1), (0, 1), (1, -1), (1, 0), (1, 1))
SIDE_TABLE = (
    ((0, 0), (3, 1), (1, 3), (2, 2)),
    ((1, 0), (2, 1), (0, 3), (3, 2)),
    ((2, 0), (0, 2), (3, 3), (1, 1)),
    ((3, 0), (1, 2), (2, 3), (0, 1)),
)
SIDE_DIRECTION = (1, 6, 3, 4)
SIDE_ENDS = ((0, 2), (5, 7))
SIDE_TAPS = (((0, 0), (0, 1), (0, 2)), ((2, 0), (2, 1), (2, 2)), ((0, 0), (1, 0), (2, 0)), ((0, 2), (1, 2), (2, 2)))


def wanted_side(row_step, col_step):
    if row_step < 0:
        return 1
    if row_step > 0:
        return 0
    return 3 if col_step < 0 else 2


def flip_tables(length):
    size = 2 * length
    flips = np.zeros((4, size, size), np.float32)
    for code in range(4):
        for r in range(2):
            for k in range(length):
                rr = 1 - r if code & 1 else r
                kk = length - 1 - k if code & 2 else k
                flips[code, r * length + k, rr * length + kk] = 1
    back = np.zeros((2, size, size), np.float32)
    ahead = np.zeros((2, size, size), np.float32)
    for r in range(2):
        for k in range(length):
            back[int(k < 2), r * length + k, r * length + (k - 2) % length] = 1
            ahead[int(k >= length - 2), r * length + k, r * length + (k + 2) % length] = 1
    sides = np.stack([np.concatenate([back[0] @ f, f, ahead[0] @ f]) for f in flips])
    ends = np.stack([np.concatenate([back[1] @ f, ahead[1] @ f]) for f in flips])
    return flips, sides, ends


def place_of(me, neighbour, rotation, which, patches_here, devices):
    owner = lax.div(neighbour, patches_here)
    within = neighbour - owner * patches_here
    offset = owner - me
    offset = jnp.where(offset < 0, offset + devices, offset)
    core = lax.rem(me, 2)
    to_mate = jnp.where(core == 0, 1, devices - 1)
    block = jnp.where(offset == to_mate, 3, 4)
    block = jnp.where(offset == 2, 2, block)
    block = jnp.where(offset == devices - 2, 1, block)
    block = jnp.where(offset == 0, 0, block)
    slot, code = SIDE_TABLE[which][0]
    for k in range(1, 4):
        slot = jnp.where(rotation == k, SIDE_TABLE[which][k][0], slot)
        code = jnp.where(rotation == k, SIDE_TABLE[which][k][1], code)
    return (block * patches_here + within) * 4 + slot, code


def dot(a, b):
    return jnp.dot(a, b, preferred_element_type=F32)


def column_strip(wide_ref, first, length):
    return jnp.concatenate([wide_ref[pl.ds(first + c, length, stride=length), :] for c in range(2)], axis=0)


def add_columns(wide_ref, first, length, strip):
    for c in range(2):
        at = pl.ds(first + c, length, stride=length)
        wide_ref[at, :] = wide_ref[at, :] + strip[c * length : (c + 1) * length]


def spread(ext_ref, wide, length):
    count = length * length
    column = lax.broadcasted_iota(jnp.int32, (count, 1), 0) & (length - 1)
    pad = 2 * length
    back = jnp.where(column >= 2, pltpu.roll(wide, 2, 0), 0.0)
    ahead = jnp.where(column < length - 2, pltpu.roll(wide, count - 2, 0), 0.0)
    ext_ref[pad : pad + count, 0:128] = back.astype(BF)
    ext_ref[pad : pad + count, 128:256] = wide.astype(BF)
    ext_ref[pad : pad + count, 256:384] = ahead.astype(BF)


def clear_rows(ext_ref, length):
    pad = 2 * length
    empty = jnp.zeros((pad, 384), BF)
    ext_ref[0:pad, :] = empty
    ext_ref[pad + length * length :, :] = empty


def begin(source, target, sem):
    copy = pltpu.make_async_copy(source, target, sem)
    copy.start()
    return copy


def finish(copies):
    for copy in copies:
        copy.wait()


def pack_kernel(x_ref, out_ref, x_vm, out_vm, wide_ref, sems, *, length):
    count = length * length
    patches = x_vm.shape[0]
    arriving = [begin(x_ref.at[p], x_vm.at[p], sems.at[p]) for p in range(patches)]
    leaving = []
    for p in range(patches):
        arriving[p].wait()
        out_vm[4 * p] = x_vm[p, 0 : 2 * length, :]
        out_vm[4 * p + 1] = x_vm[p, count - 2 * length :, :]
        wide_ref[...] = x_vm[p].astype(F32)
        out_vm[4 * p + 2] = column_strip(wide_ref, 0, length).astype(BF)
        out_vm[4 * p + 3] = column_strip(wide_ref, length - 2, length).astype(BF)
        rows = pl.ds(4 * p, 4)
        leaving.append(begin(out_vm.at[rows], out_ref.at[rows], sems.at[patches + p]))
    finish(leaving)


def own_kernel(
    me_ref, nb_ref, rot_ref, cor_ref, x_ref, cot_ref, w_ref, bias_in_ref, flip_ref,
    strips_ref, own_ref, far_ref, near_ref, dw_ref, dx_ref, mid_ref,
    nb_sm, rot_sm, cor_sm, x_vm, cot_vm, w_vm, bias_in_vm, flip_vm,
    strips_vm, near_vm, dw_vm, dx_vm, mid_vm, ext_ref, wide_ref, pool_ref, sems, *, length, devices,
):
    patches = x_vm.shape[0]
    count = length * length
    size = 2 * length
    block = 4 * patches
    chunk = min(count, 256)
    sources = [nb_ref, rot_ref, cor_ref, w_ref, bias_in_ref, flip_ref]
    targets = [nb_sm, rot_sm, cor_sm, w_vm, bias_in_vm, flip_vm]
    arriving = [begin(a, b, sems.at[i]) for i, (a, b) in enumerate(zip(sources, targets))]
    used = len(arriving)
    cots = [begin(cot_ref.at[p], cot_vm.at[p], sems.at[used + p]) for p in range(patches)]
    used += patches
    xs = [begin(x_ref.at[p], x_vm.at[p], sems.at[used + p]) for p in range(patches)]
    used += patches
    leaving = []
    me = me_ref[0]
    pool_ref[...] = jnp.zeros_like(pool_ref)
    clear_rows(ext_ref, length)
    along = lax.broadcasted_iota(jnp.int32, (length, 1), 0)
    finish(arriving)
    taps = [jnp.concatenate([w_vm[a * 3 + b] for a, b in SIDE_TAPS[s]], axis=0) for s in range(4)]
    for p in range(patches):
        cots[p].wait()
        wide_ref[...] = cot_vm[p].astype(F32)
        strips = [
            cot_vm[p, 0:size, :],
            cot_vm[p, count - size :, :],
            column_strip(wide_ref, 0, length).astype(BF),
            column_strip(wide_ref, length - 2, length).astype(BF),
        ]
        for s in range(4):
            strips_vm[s, size * p : size * (p + 1), :] = strips[s]
            terms = lax.dot_general(strips[s], taps[s], (((1,), (1,)), ((), ())), preferred_element_type=F32)
            side, first, last = [], [], []
            for r in range(2):
                rows = slice(r * length, (r + 1) * length)
                ahead = pltpu.roll(terms[rows, 0:128], length - 2, 0)
                back = pltpu.roll(terms[rows, 256:384], 2, 0)
                side.append(
                    terms[rows, 128:256]
                    + jnp.where(along < length - 2, ahead, 0.0)
                    + jnp.where(along >= 2, back, 0.0)
                )
                first.append(jnp.where(along >= length - 2, ahead, 0.0))
                last.append(jnp.where(along < 2, back, 0.0))
            sent = [(SIDE_DIRECTION[s], side)]
            if s < 2:
                sent += [(SIDE_ENDS[s][0], first), (SIDE_ENDS[s][1], last)]
            for j, term in sent:
                where_to, code = place_of(
                    me, nb_sm[p, j], rot_sm[p, j], wanted_side(*DIRECTIONS[j]), patches, devices
                )
                value = dot(flip_vm[code], jnp.concatenate(term, axis=0).astype(BF))
                value = value * (cor_sm[p, j] > 0).astype(F32)
                pool_ref[where_to] = pool_ref[where_to] + value
    near_vm[...] = pool_ref[3 * block :].astype(BF)
    for source, target in (
        (strips_vm, strips_ref), (near_vm, near_ref),
        (pool_ref.at[pl.ds(0, block)], own_ref), (pool_ref.at[pl.ds(block, 2 * block)], far_ref),
    ):
        leaving.append(begin(source, target, sems.at[used]))
        used += 1

    total_bias = jnp.zeros((1, 128), F32)
    flipped = [
        jnp.concatenate([w_vm[(2 - a) * 3 + 2], w_vm[(2 - a) * 3 + 1], w_vm[(2 - a) * 3]], axis=1) for a in range(3)
    ]
    rows_of = [jnp.concatenate([w_vm[a * 3 + b] for b in range(3)], axis=0) for a in range(3)]
    for p in range(patches):
        wide = cot_vm[p].astype(F32)
        total_bias = total_bias + jnp.sum(wide, axis=0, keepdims=True)
        spread(ext_ref, wide, length)
        xs[p].wait()
        turned = x_vm[p].T
        for a in range(3):
            grads = dot(turned, ext_ref[size * a : size * a + count, :])
            for b in range(3):
                tap = (2 - a) * 3 + 2 - b
                rows = slice(tap * 128, (tap + 1) * 128)
                part = grads[:, b * 128 : (b + 1) * 128]
                dw_vm[rows, :] = part if p == 0 else dw_vm[rows, :] + part
        for start in range(0, count, chunk):
            total = None
            for a in range(3):
                at = start + size * a
                part = lax.dot_general(
                    ext_ref[at : at + chunk, :], flipped[a], (((1,), (1,)), ((), ())), preferred_element_type=F32
                )
                total = part if total is None else total + part
            dx_vm[p, start : start + chunk, :] = total.astype(BF)
        leaving.append(begin(dx_vm.at[p], dx_ref.at[p], sems.at[used]))
        used += 1
    dw_vm[9 * 128 :, :] = jnp.zeros((dw_vm.shape[0] - 9 * 128, 128), F32)
    dw_vm[9 * 128 : 9 * 128 + 8, :] = jnp.broadcast_to(total_bias, (8, 128))
    leaving.append(begin(dw_vm, dw_ref, sems.at[used]))
    used += 1
    for p in range(patches):
        spread(ext_ref, x_vm[p].astype(F32), length)
        for start in range(0, count, chunk):
            total = jnp.broadcast_to(bias_in_vm[...], (chunk, 128))
            for a in range(3):
                at = start + size * a
                total = total + dot(ext_ref[at : at + chunk, :], rows_of[a])
            mid_vm[p, start : start + chunk, :] = total
        leaving.append(begin(mid_vm.at[p], mid_ref.at[p], sems.at[used]))
        used += 1
    finish(leaving)


def halo_kernel(
    me_ref, nb_ref, rot_ref, cor_ref, own_ref, low_ref, high_ref, mate_ref, across_ref, strips_ref, dw_ref,
    side_ref, end_ref, keep_ref, send_ref, halo_ref,
    nb_sm, rot_sm, cor_sm, pool_ref, strips_vm, total_ref, side_vm, end_vm, halo_vm, sems, *, length, devices, factor,
):
    block = pool_ref.shape[0] // 5
    patches = block // 4
    sources = [nb_ref, rot_ref, cor_ref, side_ref, end_ref]
    targets = [nb_sm, rot_sm, cor_sm, side_vm, end_vm]
    arriving = [begin(a, b, sems.at[i]) for i, (a, b) in enumerate(zip(sources, targets))]
    used = len(arriving)
    later = [begin(strips_ref, strips_vm, sems.at[used]), begin(dw_ref, total_ref, sems.at[used + 1])]
    used += 2
    for i, source in enumerate((own_ref, low_ref, high_ref, mate_ref, across_ref)):
        pool_ref[i * block : (i + 1) * block] = source[...]
    me = me_ref[0]
    size = 2 * length
    finish(arriving)
    for p in range(patches):

        def fetch(j):
            at, code = place_of(me, nb_sm[p, j], rot_sm[p, j], wanted_side(*DIRECTIONS[j]), patches, devices)
            return pool_ref[at], code

        for s in range(4):
            source, code = fetch(SIDE_DIRECTION[s])
            shifted = dot(side_vm[code], source)
            parts = [shifted[0:size], shifted[size : 2 * size], shifted[2 * size :]]
            if s < 2:
                for which, j in ((0, SIDE_ENDS[s][0]), (1, SIDE_ENDS[s][1])):
                    source, code = fetch(j)
                    corner = dot(end_vm[code, which * size : (which + 1) * size, :], source)
                    parts[2 * which] = parts[2 * which] + corner * (cor_sm[p, j] > 0).astype(F32)
            for i in range(3):
                halo_vm[s, p * size : (p + 1) * size, i * 128 : (i + 1) * 128] = parts[i].astype(BF)
    leaving = [begin(halo_vm, halo_ref, sems.at[used])]
    finish(later)
    for s in range(4):
        grads = lax.dot_general(
            halo_vm[s], strips_vm[s], (((0,), (0,)), ((), ())), preferred_element_type=F32
        )
        for i, (a, b) in enumerate(SIDE_TAPS[s]):
            rows = slice((a * 3 + b) * 128, (a * 3 + b + 1) * 128)
            total_ref[rows, :] = total_ref[rows, :] + grads[i * 128 : (i + 1) * 128]
    half = total_ref.shape[0] // 2
    core = lax.rem(me, 2)
    send_ref[...] = total_ref[pl.ds(pl.multiple_of((1 - core) * half, 128), half), :] * factor
    keep_ref[...] = total_ref[pl.ds(pl.multiple_of(core * half, 128), half), :] * factor
    finish(leaving)


def forward_kernel(mid_ref, w_ref, halo_ref, out_ref, mid_vm, w_vm, halo_vm, out_vm, sems, *, length):
    count = length * length
    size = 2 * length
    patches = mid_vm.shape[0]
    arriving = [begin(w_ref, w_vm, sems.at[0]), begin(halo_ref, halo_vm, sems.at[1])]
    mids = [begin(mid_ref.at[p], mid_vm.at[p], sems.at[2 + p]) for p in range(patches)]
    finish(arriving)
    borders = []
    for s in range(4):
        taps = jnp.concatenate([w_vm[a * 3 + b] for a, b in SIDE_TAPS[s]], axis=0)
        borders.append(dot(halo_vm[s], taps))
    leaving = []
    for p in range(patches):
        mids[p].wait()
        mine = slice(p * size, (p + 1) * size)
        wide_ref = mid_vm.at[p]
        wide_ref[0:size, :] = wide_ref[0:size, :] + borders[0][mine]
        wide_ref[count - size :, :] = wide_ref[count - size :, :] + borders[1][mine]
        add_columns(wide_ref, 0, length, borders[2][mine])
        add_columns(wide_ref, length - 2, length, borders[3][mine])
        out_vm[p] = wide_ref[...].astype(BF)
        leaving.append(begin(out_vm.at[p], out_ref.at[p], sems.at[2 + patches + p]))
    finish(leaving)


def join_kernel(
    dx_ref, own_ref, near_ref, low_ref, high_ref, out_ref,
    dx_vm, own_vm, out_vm, wide_ref, sems, *, length,
):
    count = length * length
    size = 2 * length
    patches = dx_vm.shape[0]
    arriving = [begin(own_ref, own_vm, sems.at[0])]
    used = len(arriving)
    dxs = [begin(dx_ref.at[p], dx_vm.at[p], sems.at[used + p]) for p in range(patches)]
    used += patches
    finish(arriving)
    leaving = []
    for p in range(patches):
        dxs[p].wait()
        wide_ref[...] = dx_vm[p].astype(F32)
        strips = []
        for s in range(4):
            i = 4 * p + s
            strips.append(own_vm[i] + near_ref[i].astype(F32) + low_ref[i].astype(F32) + high_ref[i].astype(F32))
        wide_ref[0:size, :] = wide_ref[0:size, :] + strips[0]
        wide_ref[count - size :, :] = wide_ref[count - size :, :] + strips[1]
        add_columns(wide_ref, 0, length, strips[2])
        add_columns(wide_ref, length - 2, length, strips[3])
        out_vm[p] = wide_ref[...].astype(BF)
        leaving.append(begin(out_vm.at[p], out_ref.at[p], sems.at[used]))
        used += 1
    finish(leaving)


def result_kernel(me_ref, mine_ref, other_ref, grad_ref, bias_ref, sems, *, taps):
    core = lax.rem(me_ref[0], 2)
    half = mine_ref.shape[0]
    rest = taps - half

    def write(low_ref, high_ref):
        leaving = [
            begin(low_ref, grad_ref.at[pl.ds(0, half)], sems.at[0]),
            begin(high_ref.at[pl.ds(0, rest)], grad_ref.at[pl.ds(half, rest)], sems.at[1]),
        ]
        bias_ref[...] = high_ref[rest : rest + 1, :]
        finish(leaving)

    @pl.when(core == 0)
    def _():
        write(mine_ref, other_ref)

    @pl.when(core == 1)
    def _():
        write(other_ref, mine_ref)


def call(kernel, name, operands, outs, scratch, copies, small=(), room=4):
    spaces = {"s": pltpu.SMEM, "h": pltpu.HBM, "a": pl.ANY, "v": pltpu.VMEM}
    out_specs = [pl.BlockSpec(memory_space=pltpu.VMEM if i in small else pl.ANY) for i in range(len(outs))]
    return pl.pallas_call(
        kernel,
        name=name,
        out_shape=list(outs),
        in_specs=[pl.BlockSpec(memory_space=spaces[o]) for o in operands],
        out_specs=out_specs,
        scratch_shapes=list(scratch) + [pltpu.SemaphoreType.DMA((copies,))],
        compiler_params=pltpu.CompilerParams(vmem_limit_bytes=(64 - room) * 1024 * 1024),
        cost_estimate=pl.CostEstimate(flops=0, bytes_accessed=0, transcendentals=0),
    )


def shifted(value, steps):
    count = lax.axis_size("patch")
    return lax.ppermute(value, "patch", [(d, (d + steps) % count) for d in range(count)])


def swapped(value, mask):
    return lax.ppermute(value, "patch", [(d, d ^ mask) for d in range(lax.axis_size("patch"))])


def part_of(value, index, size):
    return lax.dynamic_slice_in_dim(value, index * size, size)


def summed(keep, send, me, devices, between, last):
    mine = keep + swapped(send, 1)
    quarter = mine.shape[0] // 4
    at = (me // 2) % 4
    arrived = [swapped(part_of(mine, at ^ k, quarter).astype(BF), 2 * k) for k in range(1, 4)]
    mine = part_of(mine, at, quarter)
    for a in arrived:
        mine = mine + a.astype(F32)
    step = 8
    while step < devices:
        sent = mine.astype(BF)
        arrived = [swapped(sent, k * step) for k in range(1, 4 if 2 * step < devices else 2)]
        if 4 * step >= devices:
            arrived = between(arrived)
        mine = sent.astype(F32) + arrived[0].astype(F32)
        if len(arrived) > 1:
            mine = mine + (arrived[1].astype(F32) + arrived[2].astype(F32))
        step *= 4
    pieces = jnp.stack([mine] + [swapped(mine, 2 * k) for k in range(1, 4)])
    whole = jnp.concatenate([lax.dynamic_index_in_dim(pieces, at ^ k, 0, False) for k in range(4)])
    whole = last(whole)
    return whole, swapped(whole, 1)


def body(inputs, cotangent, weights, bias_vector, neighbours, rotations, corners):
    patches, length, _, chans = inputs.shape
    devices = lax.axis_size("patch")
    count = length * length
    size = 2 * length
    block = 4 * patches
    rows = 10 * chans
    me = lax.axis_index("patch")
    me_arr = me.reshape(1).astype(jnp.int32)
    core = me % 2
    x = inputs.reshape(patches, count, chans)
    cot = cotangent.reshape(patches, count, chans)
    w = weights.reshape(9, chans, chans)
    flips, sides, ends = (jnp.asarray(t, BF) for t in flip_tables(length))
    shape = jax.ShapeDtypeStruct
    scratch = pltpu.VMEM
    tables = (me_arr, neighbours, rotations, corners)
    table_scratch = [pltpu.SMEM(neighbours.shape, jnp.int32)] * 3

    (edges,) = call(
        functools.partial(pack_kernel, length=length), "pack_edges", "h", [shape((block, size, chans), BF)],
        [scratch(x.shape, BF), scratch((block, size, chans), BF), scratch((count, chans), F32)], 2 * patches,
    )(x)
    from_low = shifted(edges, 2)
    from_high = shifted(edges, -2)
    from_mate = swapped(edges, 1)

    strips, own, far, near, dw, dx, mid = call(
        functools.partial(own_kernel, length=length, devices=devices), "own_pixels", "shhhhhhhh",
        [
            shape((4, patches * size, chans), BF),
            shape((block, size, chans), F32),
            shape((2 * block, size, chans), F32),
            shape((2 * block, size, chans), BF),
            shape((rows, chans), F32),
            shape(x.shape, BF),
            shape(x.shape, F32),
        ],
        table_scratch
        + [
            scratch(x.shape, BF),
            scratch(x.shape, BF),
            scratch(w.shape, BF),
            scratch((1, chans), F32),
            scratch(flips.shape, BF),
            scratch((4, patches * size, chans), BF),
            scratch((2 * block, size, chans), BF),
            scratch((rows, chans), F32),
            scratch(x.shape, BF),
            scratch(x.shape, F32),
            scratch((count + 2 * size, 3 * chans), BF),
            scratch((count, chans), F32),
            scratch((5 * block, size, chans), F32),
        ],
        6 + 4 * patches + 5,
    )(*tables, x, cot, w, bias_vector.reshape(1, chans), flips)
    near_in = swapped(near, 1)

    from_low, from_high, dw = lax.optimization_barrier((from_low, from_high, dw))
    from_across = swapped(jnp.where(core == 0, from_high, from_low), 1)

    cross_terms = near_in[block:].astype(F32)
    to_low = (far[:block] + jnp.where(core == 1, cross_terms, 0.0)).astype(BF)
    to_high = (far[block:] + jnp.where(core == 0, cross_terms, 0.0)).astype(BF)

    factor = 1.0 / (length * math.sqrt(patches * devices))
    keep, send, halo = call(
        functools.partial(halo_kernel, length=length, devices=devices, factor=factor), "halo_kernel_grad",
        "shhhvvvvvaahh",
        [
            shape((rows // 2, chans), F32),
            shape((rows // 2, chans), F32),
            shape((4, patches * size, 3 * chans), BF),
        ],
        table_scratch
        + [
            scratch((5 * block, size, chans), BF),
            scratch(strips.shape, BF),
            scratch((rows, chans), F32),
            scratch(sides.shape, BF),
            scratch(ends.shape, BF),
            scratch((4, patches * size, 3 * chans), BF),
        ],
        8, small=(0, 1), room=ROOM,
    )(*tables, edges, from_low, from_high, from_mate, from_across, strips, dw, sides, ends)

    (outputs,) = call(
        functools.partial(forward_kernel, length=length), "add_halo_outputs", "aha", [shape(x.shape, BF)],
        [scratch(x.shape, F32), scratch(w.shape, BF), scratch(halo.shape, BF), scratch(x.shape, BF)], 2 + 2 * patches, room=ROOM,
    )(mid, w, halo)

    terms_high = shifted(to_low, -2)
    terms_low = shifted(to_high, 2)
    results = {}

    def between(value):
        value, results["high"], results["low"], results["out"] = lax.optimization_barrier(
            (value, terms_high, terms_low, outputs)
        )
        return value

    def last(value):
        (input_grad,) = call(
            functools.partial(join_kernel, length=length), "join_input_grad", "aavvv", [shape(x.shape, BF)],
            [
                scratch(x.shape, BF),
                scratch((block, size, chans), F32),
                scratch(x.shape, BF),
                scratch((count, chans), F32),
            ],
            1 + 2 * patches, room=ROOM,
        )(dx, own, near_in, results["low"], results["high"])
        value, results["in"] = lax.optimization_barrier((value, input_grad))
        return value

    mine, other = summed(keep, send, me, devices, between, last)
    weight_grad, bias_grad = call(
        functools.partial(result_kernel, taps=9 * chans), "order_kernel_grad", "svv",
        [shape((9 * chans, chans), F32), shape((1, chans), F32)], [], 2, small=(1,), room=ROOM,
    )(me_arr, mine, other)
    return (
        results["out"].reshape(inputs.shape),
        results["in"].reshape(inputs.shape),
        weight_grad.reshape(weights.shape),
        bias_grad.reshape(bias_vector.shape),
    )


def solution(mesh):
    in_specs = (
        P("patch", None, None, None),
        P("patch", None, None, None),
        P(),
        P(),
        P("patch", None),
        P("patch", None),
        P("patch", None),
    )
    out_specs = (P("patch", None, None, None), P("patch", None, None, None), P(), P())
    return jax.shard_map(body, mesh=mesh, in_specs=in_specs, out_specs=out_specs, check_vma=False)
```

```python
import functools
import math

import jax
import jax.numpy as jnp
import numpy as np
from jax import lax
from jax.experimental import pallas as pl
from jax.experimental.pallas import tpu as pltpu
from jax.sharding import PartitionSpec as P

ROOM = 12
STEP = 4
BF = jnp.bfloat16
F32 = jnp.float32

DIRECTIONS = ((-1, -1), (-1, 0), (-1, 1), (0, -1), (0, 1), (1, -1), (1, 0), (1, 1))
SIDE_TABLE = (
    ((0, 0), (3, 1), (1, 3), (2, 2)),
    ((1, 0), (2, 1), (0, 3), (3, 2)),
    ((2, 0), (0, 2), (3, 3), (1, 1)),
    ((3, 0), (1, 2), (2, 3), (0, 1)),
)
SIDE_DIRECTION = (1, 6, 3, 4)
SIDE_ENDS = ((0, 2), (5, 7))
SIDE_TAPS = (((0, 0), (0, 1), (0, 2)), ((2, 0), (2, 1), (2, 2)), ((0, 0), (1, 0), (2, 0)), ((0, 2), (1, 2), (2, 2)))


def wanted_side(row_step, col_step):
    if row_step < 0:
        return 1
    if row_step > 0:
        return 0
    return 3 if col_step < 0 else 2


def flip_tables(length):
    size = 2 * length
    flips = np.zeros((4, size, size), np.float32)
    for code in range(4):
        for r in range(2):
            for k in range(length):
                rr = 1 - r if code & 1 else r
                kk = length - 1 - k if code & 2 else k
                flips[code, r * length + k, rr * length + kk] = 1
    back = np.zeros((2, size, size), np.float32)
    ahead = np.zeros((2, size, size), np.float32)
    for r in range(2):
        for k in range(length):
            back[int(k < 2), r * length + k, r * length + (k - 2) % length] = 1
            ahead[int(k >= length - 2), r * length + k, r * length + (k + 2) % length] = 1
    sides = np.stack([np.concatenate([back[0] @ f, f, ahead[0] @ f]) for f in flips])
    ends = np.stack([np.concatenate([back[1] @ f, ahead[1] @ f]) for f in flips])
    return flips, sides, ends


def place_of(me, neighbour, rotation, which, patches_here, devices):
    owner = lax.div(neighbour, patches_here)
    within = neighbour - owner * patches_here
    offset = owner - me
    offset = jnp.where(offset < 0, offset + devices, offset)
    core = lax.rem(me, 2)
    to_mate = jnp.where(core == 0, 1, devices - 1)
    block = jnp.where(offset == to_mate, 3, 4)
    block = jnp.where(offset == 2, 2, block)
    block = jnp.where(offset == devices - 2, 1, block)
    block = jnp.where(offset == 0, 0, block)
    slot, code = SIDE_TABLE[which][0]
    for k in range(1, 4):
        slot = jnp.where(rotation == k, SIDE_TABLE[which][k][0], slot)
        code = jnp.where(rotation == k, SIDE_TABLE[which][k][1], code)
    return (block * patches_here + within) * 4 + slot, code


def dot(a, b):
    return jnp.dot(a, b, preferred_element_type=F32)


def column_strip(wide_ref, first, length):
    return jnp.concatenate([wide_ref[pl.ds(first + c, length, stride=length), :] for c in range(2)], axis=0)


def add_columns(wide_ref, first, length, strip):
    for c in range(2):
        at = pl.ds(first + c, length, stride=length)
        wide_ref[at, :] = wide_ref[at, :] + strip[c * length : (c + 1) * length]


def spread(ext_ref, wide, length):
    count = length * length
    size = 2 * length
    column = lax.broadcasted_iota(jnp.int32, (count, 1), 0) & (length - 1)
    back = jnp.where(column >= 2, pltpu.roll(wide, 2, 0), 0.0)
    ahead = jnp.where(column < length - 2, pltpu.roll(wide, count - 2, 0), 0.0)
    for i, part in enumerate((back, wide, ahead)):
        part = part.astype(BF)
        lanes = slice(i * 128, (i + 1) * 128)
        groups = count // (2 * size)
        for g in range(groups):
            at = 2 * size * g
            ext_ref[g, size:, lanes] = part[at : at + size]
            ext_ref[g + 1, 0:size, lanes] = part[at + size : at + 2 * size]


def clear_rows(ext_ref, length):
    size = 2 * length
    empty = jnp.zeros((size, 384), BF)
    ext_ref[0, 0:size, :] = empty
    ext_ref[ext_ref.shape[0] - 1, size:, :] = empty


def pair_taps(rows_of):
    none = jnp.zeros_like(rows_of[0])
    left = rows_of + [none]
    right = [none] + rows_of
    both = [jnp.concatenate([a, b], axis=1) for a, b in zip(left, right)]
    return [jnp.concatenate(both[0:2], axis=0), jnp.concatenate(both[2:4], axis=0)]


def conv_pairs(ext_ref, weights, first, groups, length):
    size = 2 * length
    total = None
    for half in range(2):
        rows = ext_ref[first + half : first + half + groups]
        pixels = jnp.concatenate(
            [rows[:, 0:size].reshape(groups * size, 384), rows[:, size:].reshape(groups * size, 384)], axis=1
        )
        part = dot(pixels, weights[half])
        total = part if total is None else total + part
    return total[:, 0:128].reshape(groups, size, 128), total[:, 128:].reshape(groups, size, 128)


def begin(source, target, sem):
    copy = pltpu.make_async_copy(source, target, sem)
    copy.start()
    return copy


def finish(copies):
    for copy in copies:
        copy.wait()


def pack_kernel(x_ref, out_vm, x_vm, wide_ref, sems, *, length):
    count = length * length
    patches = x_vm.shape[0]
    arriving = [begin(x_ref.at[p], x_vm.at[p], sems.at[p]) for p in range(patches)]
    for p in range(patches):
        arriving[p].wait()
        out_vm[4 * p] = x_vm[p, 0 : 2 * length, :]
        out_vm[4 * p + 1] = x_vm[p, count - 2 * length :, :]
        wide_ref[...] = x_vm[p].astype(F32)
        out_vm[4 * p + 2] = column_strip(wide_ref, 0, length).astype(BF)
        out_vm[4 * p + 3] = column_strip(wide_ref, length - 2, length).astype(BF)


def own_kernel(
    me_ref, nb_ref, rot_ref, cor_ref, x_ref, cot_ref, w_ref, bias_in_ref, flip_ref,
    own_ref, far_ref, near_ref, dw_ref, dx_ref, mid_ref,
    nb_sm, rot_sm, cor_sm, x_vm, cot_vm, w_vm, bias_in_vm, flip_vm,
    strips_vm, near_vm, dw_vm, dx_vm, mid_vm, ext_ref, wide_ref, pool_ref, sems, *, length, devices,
):
    patches = x_vm.shape[0]
    count = length * length
    size = 2 * length
    block = 4 * patches
    sources = [nb_ref, rot_ref, cor_ref, w_ref, bias_in_ref, flip_ref]
    targets = [nb_sm, rot_sm, cor_sm, w_vm, bias_in_vm, flip_vm]
    arriving = [begin(a, b, sems.at[i]) for i, (a, b) in enumerate(zip(sources, targets))]
    used = len(arriving)
    cots = [begin(cot_ref.at[p], cot_vm.at[p], sems.at[used + p]) for p in range(patches)]
    used += patches
    xs = [begin(x_ref.at[p], x_vm.at[p], sems.at[used + p]) for p in range(patches)]
    used += patches
    leaving = []
    me = me_ref[0]
    pool_ref[...] = jnp.zeros_like(pool_ref)
    clear_rows(ext_ref, length)
    along = lax.broadcasted_iota(jnp.int32, (length, 1), 0)
    finish(arriving)
    taps = [jnp.concatenate([w_vm[a * 3 + b] for a, b in SIDE_TAPS[s]], axis=0) for s in range(4)]
    for p in range(patches):
        cots[p].wait()
        mine = slice(size * p, size * (p + 1))
        strips_vm[0, mine, :] = cot_vm[p, 0:size, :]
        strips_vm[1, mine, :] = cot_vm[p, count - size :, :]
        wide_ref[...] = cot_vm[p].astype(F32)
        strips_vm[2, mine, :] = column_strip(wide_ref, 0, length).astype(BF)
        strips_vm[3, mine, :] = column_strip(wide_ref, length - 2, length).astype(BF)
    sent = []
    for s in range(4):
        terms = lax.dot_general(strips_vm[s], taps[s], (((1,), (1,)), ((), ())), preferred_element_type=F32)
        for p in range(patches):
            side, first, last = [], [], []
            for r in range(2):
                rows = slice(size * p + r * length, size * p + (r + 1) * length)
                ahead = pltpu.roll(terms[rows, 0:128], length - 2, 0)
                back = pltpu.roll(terms[rows, 256:384], 2, 0)
                side.append(
                    terms[rows, 128:256]
                    + jnp.where(along < length - 2, ahead, 0.0)
                    + jnp.where(along >= 2, back, 0.0)
                )
                first.append(jnp.where(along >= length - 2, ahead, 0.0))
                last.append(jnp.where(along < 2, back, 0.0))
            sent.append((p, SIDE_DIRECTION[s], side))
            if s < 2:
                sent += [(p, SIDE_ENDS[s][0], first), (p, SIDE_ENDS[s][1], last)]
    placed = []
    for p, j, term in sent:
        where_to, code = place_of(me, nb_sm[p, j], rot_sm[p, j], wanted_side(*DIRECTIONS[j]), patches, devices)
        value = dot(flip_vm[code], jnp.concatenate(term, axis=0).astype(BF))
        placed.append((where_to, value * (cor_sm[p, j] > 0).astype(F32)))
    for where_to, value in placed:
        pool_ref[where_to] = pool_ref[where_to] + value
    near_vm[...] = pool_ref[3 * block :].astype(BF)
    for source, target in (
        (near_vm, near_ref),
        (pool_ref.at[pl.ds(0, block)], own_ref), (pool_ref.at[pl.ds(block, 2 * block)], far_ref),
    ):
        leaving.append(begin(source, target, sems.at[used]))
        used += 1

    total_bias = jnp.zeros((1, 128), F32)
    flipped = pair_taps(
        [jnp.concatenate([w_vm[(2 - a) * 3 + 2 - b].T for b in range(3)], axis=0) for a in range(3)]
    )
    plain = pair_taps([jnp.concatenate([w_vm[a * 3 + b] for b in range(3)], axis=0) for a in range(3)])
    groups = count // (2 * size)
    step = min(groups, STEP)
    for p in range(patches):
        wide = cot_vm[p].astype(F32)
        total_bias = total_bias + jnp.sum(wide, axis=0, keepdims=True)
        spread(ext_ref, wide, length)
        xs[p].wait()
        turned = x_vm[p].T
        windows = [
            ext_ref[0:groups].reshape(count, 384),
            jnp.concatenate([ext_ref[0:groups, size:], ext_ref[1 : groups + 1, 0:size]], axis=1).reshape(count, 384),
            ext_ref[1 : groups + 1].reshape(count, 384),
        ]
        for a in range(3):
            grads = dot(turned, windows[a])
            for b in range(3):
                tap = (2 - a) * 3 + 2 - b
                rows = slice(tap * 128, (tap + 1) * 128)
                part = grads[:, b * 128 : (b + 1) * 128]
                dw_vm[rows, :] = part if p == 0 else dw_vm[rows, :] + part
        for g in range(0, groups, step):
            for i, part in enumerate(conv_pairs(ext_ref, flipped, g, step, length)):
                dx_vm[p, g : g + step, i * size : (i + 1) * size] = part.astype(BF)
        leaving.append(begin(dx_vm.at[p], dx_ref.at[p], sems.at[used]))
        used += 1
    dw_vm[9 * 128 : 10 * 128, :] = jnp.zeros((128, 128), F32)
    dw_vm[9 * 128 : 9 * 128 + 8, :] = jnp.broadcast_to(total_bias, (8, 128))
    for s in range(4):
        at = 10 * 128 + s * patches * size
        dw_vm[at : at + patches * size, :] = strips_vm[s].astype(F32)
    leaving.append(begin(dw_vm, dw_ref, sems.at[used]))
    used += 1
    for p in range(patches):
        spread(ext_ref, x_vm[p].astype(F32), length)
        for g in range(0, groups, step):
            for i, part in enumerate(conv_pairs(ext_ref, plain, g, step, length)):
                mid_vm[p, g : g + step, i * size : (i + 1) * size] = part + bias_in_vm[...]
        leaving.append(begin(mid_vm.at[p], mid_ref.at[p], sems.at[used]))
        used += 1
    finish(leaving)


def halo_kernel(
    me_ref, nb_ref, rot_ref, cor_ref, own_ref, low_ref, high_ref, mate_ref, across_ref, dw_ref,
    side_ref, end_ref, keep_ref, send_ref, halo_ref,
    nb_sm, rot_sm, cor_sm, pool_ref, total_ref, side_vm, end_vm, halo_vm, sems, *, length, devices, factor,
):
    block = pool_ref.shape[0] // 5
    patches = block // 4
    sources = [nb_ref, rot_ref, cor_ref, side_ref, end_ref]
    targets = [nb_sm, rot_sm, cor_sm, side_vm, end_vm]
    arriving = [begin(a, b, sems.at[i]) for i, (a, b) in enumerate(zip(sources, targets))]
    used = len(arriving)
    later = [begin(dw_ref, total_ref, sems.at[used])]
    used += 1
    for i, source in enumerate((own_ref, low_ref, high_ref, mate_ref, across_ref)):
        pool_ref[i * block : (i + 1) * block] = source[...]
    me = me_ref[0]
    size = 2 * length
    finish(arriving)
    for p in range(patches):

        def fetch(j):
            at, code = place_of(me, nb_sm[p, j], rot_sm[p, j], wanted_side(*DIRECTIONS[j]), patches, devices)
            return pool_ref[at], code

        for s in range(4):
            source, code = fetch(SIDE_DIRECTION[s])
            shifted = dot(side_vm[code], source)
            parts = [shifted[0:size], shifted[size : 2 * size], shifted[2 * size :]]
            if s < 2:
                for which, j in ((0, SIDE_ENDS[s][0]), (1, SIDE_ENDS[s][1])):
                    source, code = fetch(j)
                    corner = dot(end_vm[code, which * size : (which + 1) * size, :], source)
                    parts[2 * which] = parts[2 * which] + corner * (cor_sm[p, j] > 0).astype(F32)
            for i in range(3):
                halo_vm[s, p * size : (p + 1) * size, i * 128 : (i + 1) * 128] = parts[i].astype(BF)
    leaving = [begin(halo_vm, halo_ref, sems.at[used])]
    finish(later)
    for s in range(4):
        at = 10 * 128 + s * patches * size
        strips = total_ref[at : at + patches * size, :].astype(BF)
        grads = lax.dot_general(
            halo_vm[s], strips, (((0,), (0,)), ((), ())), preferred_element_type=F32
        )
        for i, (a, b) in enumerate(SIDE_TAPS[s]):
            rows = slice((a * 3 + b) * 128, (a * 3 + b + 1) * 128)
            total_ref[rows, :] = total_ref[rows, :] + grads[i * 128 : (i + 1) * 128]
    half = 5 * 128
    core = lax.rem(me, 2)
    send_ref[...] = total_ref[pl.ds(pl.multiple_of((1 - core) * half, 128), half), :] * factor
    keep_ref[...] = total_ref[pl.ds(pl.multiple_of(core * half, 128), half), :] * factor
    finish(leaving)


def forward_kernel(mid_ref, w_ref, halo_ref, out_ref, mid_vm, w_vm, halo_vm, out_vm, sems, *, length):
    count = length * length
    size = 2 * length
    patches = mid_vm.shape[0]
    arriving = [begin(w_ref, w_vm, sems.at[0]), begin(halo_ref, halo_vm, sems.at[1])]
    mids = [begin(mid_ref.at[p], mid_vm.at[p], sems.at[2 + p]) for p in range(patches)]
    finish(arriving)
    borders = []
    for s in range(4):
        taps = jnp.concatenate([w_vm[a * 3 + b] for a, b in SIDE_TAPS[s]], axis=0)
        borders.append(dot(halo_vm[s], taps))
    leaving = []
    for p in range(patches):
        mids[p].wait()
        mine = slice(p * size, (p + 1) * size)
        wide_ref = mid_vm.at[p]
        wide_ref[0:size, :] = wide_ref[0:size, :] + borders[0][mine]
        wide_ref[count - size :, :] = wide_ref[count - size :, :] + borders[1][mine]
        add_columns(wide_ref, 0, length, borders[2][mine])
        add_columns(wide_ref, length - 2, length, borders[3][mine])
        out_vm[p] = wide_ref[...].astype(BF)
        leaving.append(begin(out_vm.at[p], out_ref.at[p], sems.at[2 + patches + p]))
    finish(leaving)


def join_kernel(
    dx_ref, own_ref, near_ref, low_ref, high_ref, out_ref,
    dx_vm, own_vm, out_vm, wide_ref, sems, *, length,
):
    count = length * length
    size = 2 * length
    patches = dx_vm.shape[0]
    arriving = [begin(own_ref, own_vm, sems.at[0])]
    used = len(arriving)
    dxs = [begin(dx_ref.at[p], dx_vm.at[p], sems.at[used + p]) for p in range(patches)]
    used += patches
    finish(arriving)
    leaving = []
    for p in range(patches):
        dxs[p].wait()
        wide_ref[...] = dx_vm[p].astype(F32)
        strips = []
        for s in range(4):
            i = 4 * p + s
            strips.append(own_vm[i] + near_ref[i].astype(F32) + low_ref[i].astype(F32) + high_ref[i].astype(F32))
        wide_ref[0:size, :] = wide_ref[0:size, :] + strips[0]
        wide_ref[count - size :, :] = wide_ref[count - size :, :] + strips[1]
        add_columns(wide_ref, 0, length, strips[2])
        add_columns(wide_ref, length - 2, length, strips[3])
        out_vm[p] = wide_ref[...].astype(BF)
        leaving.append(begin(out_vm.at[p], out_ref.at[p], sems.at[used]))
        used += 1
    finish(leaving)


def result_kernel(me_ref, mine_ref, other_ref, grad_ref, bias_ref, sems, *, taps):
    core = lax.rem(me_ref[0], 2)
    half = mine_ref.shape[0]
    rest = taps - half

    def write(low_ref, high_ref):
        leaving = [
            begin(low_ref, grad_ref.at[pl.ds(0, half)], sems.at[0]),
            begin(high_ref.at[pl.ds(0, rest)], grad_ref.at[pl.ds(half, rest)], sems.at[1]),
        ]
        bias_ref[...] = high_ref[rest : rest + 1, :]
        finish(leaving)

    @pl.when(core == 0)
    def _():
        write(mine_ref, other_ref)

    @pl.when(core == 1)
    def _():
        write(other_ref, mine_ref)


def call(kernel, name, operands, outs, scratch, copies, small=(), room=4):
    spaces = {"s": pltpu.SMEM, "h": pltpu.HBM, "a": pl.ANY, "v": pltpu.VMEM}
    out_specs = [pl.BlockSpec(memory_space=pltpu.VMEM if i in small else pl.ANY) for i in range(len(outs))]
    return pl.pallas_call(
        kernel,
        name=name,
        out_shape=list(outs),
        in_specs=[pl.BlockSpec(memory_space=spaces[o]) for o in operands],
        out_specs=out_specs,
        scratch_shapes=list(scratch) + [pltpu.SemaphoreType.DMA((copies,))],
        compiler_params=pltpu.CompilerParams(vmem_limit_bytes=(64 - room) * 1024 * 1024),
        cost_estimate=pl.CostEstimate(flops=0, bytes_accessed=0, transcendentals=0),
    )


def shifted(value, steps):
    count = lax.axis_size("patch")
    return lax.ppermute(value, "patch", [(d, (d + steps) % count) for d in range(count)])


def swapped(value, mask):
    return lax.ppermute(value, "patch", [(d, d ^ mask) for d in range(lax.axis_size("patch"))])


def part_of(value, index, size):
    return lax.dynamic_slice_in_dim(value, index * size, size)


def summed(keep, send, me, devices, between, last):
    mine = keep + swapped(send, 1)
    quarter = mine.shape[0] // 4
    at = (me // 2) % 4
    arrived = [swapped(part_of(mine, at ^ k, quarter).astype(BF), 2 * k) for k in range(1, 4)]
    mine = part_of(mine, at, quarter)
    for a in arrived:
        mine = mine + a.astype(F32)
    step = 8
    while step < devices:
        sent = mine.astype(BF)
        arrived = [swapped(sent, k * step) for k in range(1, 4 if 2 * step < devices else 2)]
        if 4 * step >= devices:
            arrived = between(arrived)
        mine = sent.astype(F32) + arrived[0].astype(F32)
        if len(arrived) > 1:
            mine = mine + (arrived[1].astype(F32) + arrived[2].astype(F32))
        step *= 4
    pieces = jnp.stack([mine] + [swapped(mine, 2 * k) for k in range(1, 4)])
    whole = jnp.concatenate([lax.dynamic_index_in_dim(pieces, at ^ k, 0, False) for k in range(4)])
    whole = last(whole)
    return whole, swapped(whole, 1)


def own_pixels(tables, x, cot, w, bias, flips, devices):
    patches, count, chans = x.shape
    length = math.isqrt(count)
    size = 2 * length
    block = 4 * patches
    rows = 10 * chans
    grouped = (patches, count // (2 * size), 2 * size, chans)
    shape = jax.ShapeDtypeStruct
    scratch = pltpu.VMEM
    table_scratch = [pltpu.SMEM(tables[1].shape, jnp.int32)] * 3
    return call(
        functools.partial(own_kernel, length=length, devices=devices), "own_pixels", "shhhhhhhh",
        [
            shape((block, size, chans), F32),
            shape((2 * block, size, chans), F32),
            shape((2 * block, size, chans), BF),
            shape((rows + block * size, chans), F32),
            shape(grouped, BF),
            shape(grouped, F32),
        ],
        table_scratch
        + [
            scratch(x.shape, BF),
            scratch(x.shape, BF),
            scratch(w.shape, BF),
            scratch((1, chans), F32),
            scratch(flips.shape, BF),
            scratch((4, patches * size, chans), BF),
            scratch((2 * block, size, chans), BF),
            scratch((rows + block * size, chans), F32),
            scratch(grouped, BF),
            scratch(grouped, F32),
            scratch((count // (2 * size) + 1, 2 * size, 3 * chans), BF),
            scratch((count, chans), F32),
            scratch((5 * block, size, chans), F32),
        ],
        6 + 4 * patches + 4,
    )(*tables, x, cot, w, bias, flips)


def body(inputs, cotangent, weights, bias_vector, neighbours, rotations, corners):
    patches, length, _, chans = inputs.shape
    devices = lax.axis_size("patch")
    count = length * length
    size = 2 * length
    block = 4 * patches
    rows = 10 * chans
    me = lax.axis_index("patch")
    me_arr = me.reshape(1).astype(jnp.int32)
    core = me % 2
    x = inputs.reshape(patches, count, chans)
    cot = cotangent.reshape(patches, count, chans)
    w = weights.reshape(9, chans, chans)
    flips, sides, ends = (jnp.asarray(t, BF) for t in flip_tables(length))
    shape = jax.ShapeDtypeStruct
    scratch = pltpu.VMEM
    tables = (me_arr, neighbours, rotations, corners)
    table_scratch = [pltpu.SMEM(neighbours.shape, jnp.int32)] * 3

    (edges,) = call(
        functools.partial(pack_kernel, length=length), "pack_edges", "h", [shape((block, size, chans), BF)],
        [scratch(x.shape, BF), scratch((count, chans), F32)], patches, small=(0,), room=ROOM,
    )(x)
    from_low = shifted(edges, 2)
    from_high = shifted(edges, -2)
    from_mate = swapped(edges, 1)

    own, far, near, dw, dx, mid = own_pixels(tables, x, cot, w, bias_vector.reshape(1, chans), flips, devices)
    dx, mid = dx.reshape(x.shape), mid.reshape(x.shape)
    near_in = swapped(near, 1)

    from_low, from_high, dw = lax.optimization_barrier((from_low, from_high, dw))
    from_across = swapped(jnp.where(core == 0, from_high, from_low), 1)

    cross_terms = near_in[block:].astype(F32)
    to_low = (far[:block] + jnp.where(core == 1, cross_terms, 0.0)).astype(BF)
    to_high = (far[block:] + jnp.where(core == 0, cross_terms, 0.0)).astype(BF)

    factor = 1.0 / (length * math.sqrt(patches * devices))
    keep, send, halo = call(
        functools.partial(halo_kernel, length=length, devices=devices, factor=factor), "halo_kernel_grad",
        "shhhvvvvvahh",
        [
            shape((rows // 2, chans), F32),
            shape((rows // 2, chans), F32),
            shape((4, patches * size, 3 * chans), BF),
        ],
        table_scratch
        + [
            scratch((5 * block, size, chans), BF),
            scratch(dw.shape, F32),
            scratch(sides.shape, BF),
            scratch(ends.shape, BF),
            scratch((4, patches * size, 3 * chans), BF),
        ],
        7, small=(0, 1), room=ROOM,
    )(*tables, edges, from_low, from_high, from_mate, from_across, dw, sides, ends)

    (outputs,) = call(
        functools.partial(forward_kernel, length=length), "add_halo_outputs", "aha", [shape(x.shape, BF)],
        [scratch(x.shape, F32), scratch(w.shape, BF), scratch(halo.shape, BF), scratch(x.shape, BF)], 2 + 2 * patches, room=ROOM,
    )(mid, w, halo)

    terms_high = shifted(to_low, -2)
    terms_low = shifted(to_high, 2)
    results = {}

    def between(value):
        value, results["high"], results["low"], results["out"] = lax.optimization_barrier(
            (value, terms_high, terms_low, outputs)
        )
        return value

    def last(value):
        (input_grad,) = call(
            functools.partial(join_kernel, length=length), "join_input_grad", "aavvv", [shape(x.shape, BF)],
            [
                scratch(x.shape, BF),
                scratch((block, size, chans), F32),
                scratch(x.shape, BF),
                scratch((count, chans), F32),
            ],
            1 + 2 * patches, room=ROOM,
        )(dx, own, near_in, results["low"], results["high"])
        value, results["in"] = lax.optimization_barrier((value, input_grad))
        return value

    mine, other = summed(keep, send, me, devices, between, last)
    weight_grad, bias_grad = call(
        functools.partial(result_kernel, taps=9 * chans), "order_kernel_grad", "svv",
        [shape((9 * chans, chans), F32), shape((1, chans), F32)], [], 2, small=(1,), room=ROOM,
    )(me_arr, mine, other)
    return (
        results["out"].reshape(inputs.shape),
        results["in"].reshape(inputs.shape),
        weight_grad.reshape(weights.shape),
        bias_grad.reshape(bias_vector.shape),
    )


def solution(mesh):
    in_specs = (
        P("patch", None, None, None),
        P("patch", None, None, None),
        P(),
        P(),
        P("patch", None),
        P("patch", None),
        P("patch", None),
    )
    out_specs = (P("patch", None, None, None), P("patch", None, None, None), P(), P())
    return jax.shard_map(body, mesh=mesh, in_specs=in_specs, out_specs=out_specs, check_vma=False)
```

```python
import functools
import math

import jax
import jax.numpy as jnp
import numpy as np
from jax import lax
from jax.experimental import pallas as pl
from jax.experimental.pallas import tpu as pltpu
from jax.sharding import PartitionSpec as P

ROOM = 12
STEP = 4
BF = jnp.bfloat16
F32 = jnp.float32

DIRECTIONS = ((-1, -1), (-1, 0), (-1, 1), (0, -1), (0, 1), (1, -1), (1, 0), (1, 1))
SIDE_TABLE = (
    ((0, 0), (3, 1), (1, 3), (2, 2)),
    ((1, 0), (2, 1), (0, 3), (3, 2)),
    ((2, 0), (0, 2), (3, 3), (1, 1)),
    ((3, 0), (1, 2), (2, 3), (0, 1)),
)
SIDE_DIRECTION = (1, 6, 3, 4)
SIDE_ENDS = ((0, 2), (5, 7))
SIDE_TAPS = (((0, 0), (0, 1), (0, 2)), ((2, 0), (2, 1), (2, 2)), ((0, 0), (1, 0), (2, 0)), ((0, 2), (1, 2), (2, 2)))


def wanted_side(row_step, col_step):
    if row_step < 0:
        return 1
    if row_step > 0:
        return 0
    return 3 if col_step < 0 else 2


def flip_tables(length):
    size = 2 * length
    flips = np.zeros((4, size, size), np.float32)
    for code in range(4):
        for r in range(2):
            for k in range(length):
                rr = 1 - r if code & 1 else r
                kk = length - 1 - k if code & 2 else k
                flips[code, r * length + k, rr * length + kk] = 1
    back = np.zeros((2, size, size), np.float32)
    ahead = np.zeros((2, size, size), np.float32)
    for r in range(2):
        for k in range(length):
            back[int(k < 2), r * length + k, r * length + (k - 2) % length] = 1
            ahead[int(k >= length - 2), r * length + k, r * length + (k + 2) % length] = 1
    sides = np.stack([np.concatenate([back[0] @ f, f, ahead[0] @ f]) for f in flips])
    ends = np.stack([np.concatenate([back[1] @ f, ahead[1] @ f]) for f in flips])
    return flips, sides, ends


def place_of(me, neighbour, rotation, which, patches_here, devices):
    owner = lax.div(neighbour, patches_here)
    within = neighbour - owner * patches_here
    offset = owner - me
    offset = jnp.where(offset < 0, offset + devices, offset)
    core = lax.rem(me, 2)
    to_mate = jnp.where(core == 0, 1, devices - 1)
    block = jnp.where(offset == to_mate, 3, 4)
    block = jnp.where(offset == 2, 2, block)
    block = jnp.where(offset == devices - 2, 1, block)
    block = jnp.where(offset == 0, 0, block)
    slot, code = SIDE_TABLE[which][0]
    for k in range(1, 4):
        slot = jnp.where(rotation == k, SIDE_TABLE[which][k][0], slot)
        code = jnp.where(rotation == k, SIDE_TABLE[which][k][1], code)
    return (block * patches_here + within) * 4 + slot, code


def dot(a, b):
    return jnp.dot(a, b, preferred_element_type=F32)


def column_strip(wide_ref, first, length):
    return jnp.concatenate([wide_ref[pl.ds(first + c, length, stride=length), :] for c in range(2)], axis=0)


def add_columns(wide_ref, first, length, strip):
    for c in range(2):
        at = pl.ds(first + c, length, stride=length)
        wide_ref[at, :] = wide_ref[at, :] + strip[c * length : (c + 1) * length]


def spread(ext_ref, wide, length):
    count = length * length
    size = 2 * length
    column = lax.broadcasted_iota(jnp.int32, (count, 1), 0) & (length - 1)
    back = jnp.where(column >= 2, pltpu.roll(wide, 2, 0), 0.0)
    ahead = jnp.where(column < length - 2, pltpu.roll(wide, count - 2, 0), 0.0)
    for i, part in enumerate((back, wide, ahead)):
        part = part.astype(BF)
        lanes = slice(i * 128, (i + 1) * 128)
        groups = count // (2 * size)
        for g in range(groups):
            at = 2 * size * g
            ext_ref[g, size:, lanes] = part[at : at + size]
            ext_ref[g + 1, 0:size, lanes] = part[at + size : at + 2 * size]


def clear_rows(ext_ref, length):
    size = 2 * length
    empty = jnp.zeros((size, 384), BF)
    ext_ref[0, 0:size, :] = empty
    ext_ref[ext_ref.shape[0] - 1, size:, :] = empty


def pair_taps(rows_of):
    none = jnp.zeros_like(rows_of[0])
    left = rows_of + [none]
    right = [none] + rows_of
    both = [jnp.concatenate([a, b], axis=1) for a, b in zip(left, right)]
    return [jnp.concatenate(both[0:2], axis=0), jnp.concatenate(both[2:4], axis=0)]


def conv_pairs(ext_ref, weights, first, groups, length):
    size = 2 * length
    total = None
    for half in range(2):
        rows = ext_ref[first + half : first + half + groups]
        pixels = jnp.concatenate(
            [rows[:, 0:size].reshape(groups * size, 384), rows[:, size:].reshape(groups * size, 384)], axis=1
        )
        part = dot(pixels, weights[half])
        total = part if total is None else total + part
    return total[:, 0:128].reshape(groups, size, 128), total[:, 128:].reshape(groups, size, 128)


def begin(source, target, sem):
    copy = pltpu.make_async_copy(source, target, sem)
    copy.start()
    return copy


def finish(copies):
    for copy in copies:
        copy.wait()


def pack_kernel(x_ref, out_vm, x_vm, wide_ref, sems, *, length):
    count = length * length
    patches = x_vm.shape[0]
    arriving = [begin(x_ref.at[p], x_vm.at[p], sems.at[p]) for p in range(patches)]
    for p in range(patches):
        arriving[p].wait()
        out_vm[4 * p] = x_vm[p, 0 : 2 * length, :]
        out_vm[4 * p + 1] = x_vm[p, count - 2 * length :, :]
        wide_ref[...] = x_vm[p].astype(F32)
        out_vm[4 * p + 2] = column_strip(wide_ref, 0, length).astype(BF)
        out_vm[4 * p + 3] = column_strip(wide_ref, length - 2, length).astype(BF)


def own_kernel(
    me_ref, nb_ref, rot_ref, cor_ref, x_ref, cot_ref, w_ref, bias_in_ref, flip_ref,
    own_ref, far_ref, near_ref, dw_ref, dx_ref, mid_ref,
    nb_sm, rot_sm, cor_sm, x_vm, cot_vm, w_vm, bias_in_vm, flip_vm,
    strips_vm, near_vm, dw_vm, dx_vm, mid_vm, ext_ref, wide_ref, pool_ref, sems, *, length, devices,
):
    patches = x_vm.shape[0]
    count = length * length
    size = 2 * length
    block = 4 * patches
    sources = [nb_ref, rot_ref, cor_ref, w_ref, bias_in_ref, flip_ref]
    targets = [nb_sm, rot_sm, cor_sm, w_vm, bias_in_vm, flip_vm]
    arriving = [begin(a, b, sems.at[i]) for i, (a, b) in enumerate(zip(sources, targets))]
    used = len(arriving)
    cots = [begin(cot_ref.at[p], cot_vm.at[p], sems.at[used + p]) for p in range(patches)]
    used += patches
    xs = [begin(x_ref.at[p], x_vm.at[p], sems.at[used + p]) for p in range(patches)]
    used += patches
    leaving = []
    me = me_ref[0]
    pool_ref[...] = jnp.zeros_like(pool_ref)
    clear_rows(ext_ref, length)
    along = lax.broadcasted_iota(jnp.int32, (length, 1), 0)
    finish(arriving)
    taps = [jnp.concatenate([w_vm[a * 3 + b] for a, b in SIDE_TAPS[s]], axis=0) for s in range(4)]
    for p in range(patches):
        cots[p].wait()
        mine = slice(size * p, size * (p + 1))
        strips_vm[0, mine, :] = cot_vm[p, 0:size, :]
        strips_vm[1, mine, :] = cot_vm[p, count - size :, :]
        wide_ref[...] = cot_vm[p].astype(F32)
        strips_vm[2, mine, :] = column_strip(wide_ref, 0, length).astype(BF)
        strips_vm[3, mine, :] = column_strip(wide_ref, length - 2, length).astype(BF)
    sent = []
    for s in range(4):
        terms = lax.dot_general(strips_vm[s], taps[s], (((1,), (1,)), ((), ())), preferred_element_type=F32)
        for p in range(patches):
            side, first, last = [], [], []
            for r in range(2):
                rows = slice(size * p + r * length, size * p + (r + 1) * length)
                ahead = pltpu.roll(terms[rows, 0:128], length - 2, 0)
                back = pltpu.roll(terms[rows, 256:384], 2, 0)
                side.append(
                    terms[rows, 128:256]
                    + jnp.where(along < length - 2, ahead, 0.0)
                    + jnp.where(along >= 2, back, 0.0)
                )
                first.append(jnp.where(along >= length - 2, ahead, 0.0))
                last.append(jnp.where(along < 2, back, 0.0))
            sent.append((p, SIDE_DIRECTION[s], side))
            if s < 2:
                sent += [(p, SIDE_ENDS[s][0], first), (p, SIDE_ENDS[s][1], last)]
    placed = []
    for p, j, term in sent:
        where_to, code = place_of(me, nb_sm[p, j], rot_sm[p, j], wanted_side(*DIRECTIONS[j]), patches, devices)
        value = dot(flip_vm[code], jnp.concatenate(term, axis=0).astype(BF))
        placed.append((where_to, value * (cor_sm[p, j] > 0).astype(F32)))
    for where_to, value in placed:
        pool_ref[where_to] = pool_ref[where_to] + value
    near_vm[...] = pool_ref[3 * block :].astype(BF)
    for source, target in (
        (near_vm, near_ref),
        (pool_ref.at[pl.ds(0, block)], own_ref), (pool_ref.at[pl.ds(block, 2 * block)], far_ref),
    ):
        leaving.append(begin(source, target, sems.at[used]))
        used += 1

    total_bias = jnp.zeros((1, 128), F32)
    flipped = pair_taps(
        [jnp.concatenate([w_vm[(2 - a) * 3 + 2 - b].T for b in range(3)], axis=0) for a in range(3)]
    )
    plain = pair_taps([jnp.concatenate([w_vm[a * 3 + b] for b in range(3)], axis=0) for a in range(3)])
    groups = count // (2 * size)
    step = min(groups, STEP)
    for p in range(patches):
        wide = cot_vm[p].astype(F32)
        total_bias = total_bias + jnp.sum(wide, axis=0, keepdims=True)
        spread(ext_ref, wide, length)
        xs[p].wait()
        turned = x_vm[p].T
        windows = [
            ext_ref[0:groups].reshape(count, 384),
            jnp.concatenate([ext_ref[0:groups, size:], ext_ref[1 : groups + 1, 0:size]], axis=1).reshape(count, 384),
            ext_ref[1 : groups + 1].reshape(count, 384),
        ]
        for a in range(3):
            grads = dot(turned, windows[a])
            for b in range(3):
                tap = (2 - a) * 3 + 2 - b
                rows = slice(tap * 128, (tap + 1) * 128)
                part = grads[:, b * 128 : (b + 1) * 128]
                dw_vm[rows, :] = part if p == 0 else dw_vm[rows, :] + part
        for g in range(0, groups, step):
            for i, part in enumerate(conv_pairs(ext_ref, flipped, g, step, length)):
                dx_vm[p, g : g + step, i * size : (i + 1) * size] = part.astype(BF)
        leaving.append(begin(dx_vm.at[p], dx_ref.at[p], sems.at[used]))
        used += 1
    dw_vm[9 * 128 : 10 * 128, :] = jnp.zeros((128, 128), F32)
    dw_vm[9 * 128 : 9 * 128 + 8, :] = jnp.broadcast_to(total_bias, (8, 128))
    for s in range(4):
        at = 10 * 128 + s * patches * size
        dw_vm[at : at + patches * size, :] = strips_vm[s].astype(F32)
    leaving.append(begin(dw_vm, dw_ref, sems.at[used]))
    used += 1
    for p in range(patches):
        spread(ext_ref, x_vm[p].astype(F32), length)
        for g in range(0, groups, step):
            for i, part in enumerate(conv_pairs(ext_ref, plain, g, step, length)):
                mid_vm[p, g : g + step, i * size : (i + 1) * size] = part + bias_in_vm[...]
        leaving.append(begin(mid_vm.at[p], mid_ref.at[p], sems.at[used]))
        used += 1
    finish(leaving)


def halo_kernel(
    me_ref, nb_ref, rot_ref, cor_ref, own_ref, low_ref, high_ref, mate_ref, across_ref, dw_ref,
    side_ref, end_ref, keep_ref, send_ref, halo_ref,
    nb_sm, rot_sm, cor_sm, pool_ref, total_ref, side_vm, end_vm, halo_vm, sems, *, length, devices, factor,
):
    block = pool_ref.shape[0] // 5
    patches = block // 4
    sources = [nb_ref, rot_ref, cor_ref, side_ref, end_ref]
    targets = [nb_sm, rot_sm, cor_sm, side_vm, end_vm]
    arriving = [begin(a, b, sems.at[i]) for i, (a, b) in enumerate(zip(sources, targets))]
    used = len(arriving)
    later = [begin(dw_ref, total_ref, sems.at[used])]
    used += 1
    for i, source in enumerate((own_ref, low_ref, high_ref, mate_ref, across_ref)):
        pool_ref[i * block : (i + 1) * block] = source[...]
    me = me_ref[0]
    size = 2 * length
    finish(arriving)
    for p in range(patches):

        def fetch(j):
            at, code = place_of(me, nb_sm[p, j], rot_sm[p, j], wanted_side(*DIRECTIONS[j]), patches, devices)
            return pool_ref[at], code

        for s in range(4):
            source, code = fetch(SIDE_DIRECTION[s])
            shifted = dot(side_vm[code], source)
            parts = [shifted[0:size], shifted[size : 2 * size], shifted[2 * size :]]
            if s < 2:
                for which, j in ((0, SIDE_ENDS[s][0]), (1, SIDE_ENDS[s][1])):
                    source, code = fetch(j)
                    corner = dot(end_vm[code, which * size : (which + 1) * size, :], source)
                    parts[2 * which] = parts[2 * which] + corner * (cor_sm[p, j] > 0).astype(F32)
            for i in range(3):
                halo_vm[s, p * size : (p + 1) * size, i * 128 : (i + 1) * 128] = parts[i].astype(BF)
    leaving = [begin(halo_vm, halo_ref, sems.at[used])]
    finish(later)
    for s in range(4):
        at = 10 * 128 + s * patches * size
        strips = total_ref[at : at + patches * size, :].astype(BF)
        grads = lax.dot_general(
            halo_vm[s], strips, (((0,), (0,)), ((), ())), preferred_element_type=F32
        )
        for i, (a, b) in enumerate(SIDE_TAPS[s]):
            rows = slice((a * 3 + b) * 128, (a * 3 + b + 1) * 128)
            total_ref[rows, :] = total_ref[rows, :] + grads[i * 128 : (i + 1) * 128]
    taps = 9 * 128
    half = taps // 2
    core = lax.rem(me, 2)
    for target, which in ((send_ref, 1 - core), (keep_ref, core)):
        target[0:half, :] = total_ref[pl.ds(pl.multiple_of(which * half, 64), half), :] * factor
        target[half:, :] = total_ref[taps : taps + target.shape[0] - half, :] * factor
    finish(leaving)


def forward_kernel(mid_ref, w_ref, halo_ref, out_ref, mid_vm, w_vm, halo_vm, out_vm, sems, *, length):
    count = length * length
    size = 2 * length
    patches = mid_vm.shape[0]
    arriving = [begin(w_ref, w_vm, sems.at[0]), begin(halo_ref, halo_vm, sems.at[1])]
    mids = [begin(mid_ref.at[p], mid_vm.at[p], sems.at[2 + p]) for p in range(patches)]
    finish(arriving)
    borders = []
    for s in range(4):
        taps = jnp.concatenate([w_vm[a * 3 + b] for a, b in SIDE_TAPS[s]], axis=0)
        borders.append(dot(halo_vm[s], taps))
    leaving = []
    for p in range(patches):
        mids[p].wait()
        mine = slice(p * size, (p + 1) * size)
        wide_ref = mid_vm.at[p]
        wide_ref[0:size, :] = wide_ref[0:size, :] + borders[0][mine]
        wide_ref[count - size :, :] = wide_ref[count - size :, :] + borders[1][mine]
        add_columns(wide_ref, 0, length, borders[2][mine])
        add_columns(wide_ref, length - 2, length, borders[3][mine])
        out_vm[p] = wide_ref[...].astype(BF)
        leaving.append(begin(out_vm.at[p], out_ref.at[p], sems.at[2 + patches + p]))
    finish(leaving)


def join_kernel(
    dx_ref, own_ref, near_ref, low_ref, high_ref, out_ref,
    dx_vm, own_vm, out_vm, wide_ref, sems, *, length,
):
    count = length * length
    size = 2 * length
    patches = dx_vm.shape[0]
    arriving = [begin(own_ref, own_vm, sems.at[0])]
    used = len(arriving)
    dxs = [begin(dx_ref.at[p], dx_vm.at[p], sems.at[used + p]) for p in range(patches)]
    used += patches
    finish(arriving)
    leaving = []
    for p in range(patches):
        dxs[p].wait()
        wide_ref[...] = dx_vm[p].astype(F32)
        strips = []
        for s in range(4):
            i = 4 * p + s
            strips.append(own_vm[i] + near_ref[i].astype(F32) + low_ref[i].astype(F32) + high_ref[i].astype(F32))
        wide_ref[0:size, :] = wide_ref[0:size, :] + strips[0]
        wide_ref[count - size :, :] = wide_ref[count - size :, :] + strips[1]
        add_columns(wide_ref, 0, length, strips[2])
        add_columns(wide_ref, length - 2, length, strips[3])
        out_vm[p] = wide_ref[...].astype(BF)
        leaving.append(begin(out_vm.at[p], out_ref.at[p], sems.at[used]))
        used += 1
    finish(leaving)


def half_kernel(me_ref, half_ref, *refs, mates):
    grad_ref, sem = refs[1 if mates else 0], refs[-1]
    half = grad_ref.shape[0] // 2
    core = lax.rem(me_ref[0], 2)
    at = (1 - core) * half if mates else core * half
    copy = begin(half_ref.at[pl.ds(0, half)], grad_ref.at[pl.ds(pl.multiple_of(at, 64), half)], sem.at[0])
    if not mates:
        bias_ref = refs[1]
        bias_ref[...] = half_ref[half : half + 1, :]
    copy.wait()


def call(kernel, name, operands, outs, scratch, copies, small=(), room=4, aliases=None):
    spaces = {"s": pltpu.SMEM, "h": pltpu.HBM, "a": pl.ANY, "v": pltpu.VMEM}
    out_specs = [pl.BlockSpec(memory_space=pltpu.VMEM if i in small else pl.ANY) for i in range(len(outs))]
    return pl.pallas_call(
        kernel,
        name=name,
        out_shape=list(outs),
        input_output_aliases=aliases or {},
        in_specs=[pl.BlockSpec(memory_space=spaces[o]) for o in operands],
        out_specs=out_specs,
        scratch_shapes=list(scratch) + [pltpu.SemaphoreType.DMA((copies,))],
        compiler_params=pltpu.CompilerParams(vmem_limit_bytes=(64 - room) * 1024 * 1024),
        cost_estimate=pl.CostEstimate(flops=0, bytes_accessed=0, transcendentals=0),
    )


def shifted(value, steps):
    count = lax.axis_size("patch")
    return lax.ppermute(value, "patch", [(d, (d + steps) % count) for d in range(count)])


def swapped(value, mask):
    return lax.ppermute(value, "patch", [(d, d ^ mask) for d in range(lax.axis_size("patch"))])


def part_of(value, index, size):
    return lax.dynamic_slice_in_dim(value, index * size, size)


def summed(keep, send, me, devices, between, last):
    mine = keep + swapped(send, 1)
    quarter = mine.shape[0] // 4
    at = (me // 2) % 4
    arrived = [swapped(part_of(mine, at ^ k, quarter).astype(BF), 2 * k) for k in (3, 2, 1)]
    mine = part_of(mine, at, quarter)
    for a in arrived:
        mine = mine + a.astype(F32)
    step = 8
    while step < devices:
        sent = mine.astype(BF)
        arrived = [swapped(sent, k * step) for k in range(1, 4 if 2 * step < devices else 2)]
        if 4 * step >= devices:
            arrived = between(arrived)
        mine = sent.astype(F32) + arrived[0].astype(F32)
        if len(arrived) > 1:
            mine = mine + (arrived[1].astype(F32) + arrived[2].astype(F32))
        step *= 4
    pieces = jnp.stack([mine] + [swapped(mine, 2 * k) for k in range(1, 4)])
    whole = jnp.concatenate([lax.dynamic_index_in_dim(pieces, at ^ k, 0, False) for k in range(4)])
    whole = last(whole)
    return whole, swapped(whole, 1)


def own_pixels(tables, x, cot, w, bias, flips, devices):
    patches, count, chans = x.shape
    length = math.isqrt(count)
    size = 2 * length
    block = 4 * patches
    rows = 10 * chans
    grouped = (patches, count // (2 * size), 2 * size, chans)
    shape = jax.ShapeDtypeStruct
    scratch = pltpu.VMEM
    table_scratch = [pltpu.SMEM(tables[1].shape, jnp.int32)] * 3
    return call(
        functools.partial(own_kernel, length=length, devices=devices), "own_pixels", "shhhhhhhh",
        [
            shape((block, size, chans), F32),
            shape((2 * block, size, chans), F32),
            shape((2 * block, size, chans), BF),
            shape((rows + block * size, chans), F32),
            shape(grouped, BF),
            shape(grouped, F32),
        ],
        table_scratch
        + [
            scratch(x.shape, BF),
            scratch(x.shape, BF),
            scratch(w.shape, BF),
            scratch((1, chans), F32),
            scratch(flips.shape, BF),
            scratch((4, patches * size, chans), BF),
            scratch((2 * block, size, chans), BF),
            scratch((rows + block * size, chans), F32),
            scratch(grouped, BF),
            scratch(grouped, F32),
            scratch((count // (2 * size) + 1, 2 * size, 3 * chans), BF),
            scratch((count, chans), F32),
            scratch((5 * block, size, chans), F32),
        ],
        6 + 4 * patches + 4,
    )(*tables, x, cot, w, bias, flips)


def body(inputs, cotangent, weights, bias_vector, neighbours, rotations, corners):
    patches, length, _, chans = inputs.shape
    devices = lax.axis_size("patch")
    count = length * length
    size = 2 * length
    block = 4 * patches
    rows = 10 * chans
    me = lax.axis_index("patch")
    me_arr = me.reshape(1).astype(jnp.int32)
    core = me % 2
    x = inputs.reshape(patches, count, chans)
    cot = cotangent.reshape(patches, count, chans)
    w = weights.reshape(9, chans, chans)
    flips, sides, ends = (jnp.asarray(t, BF) for t in flip_tables(length))
    shape = jax.ShapeDtypeStruct
    scratch = pltpu.VMEM
    tables = (me_arr, neighbours, rotations, corners)
    table_scratch = [pltpu.SMEM(neighbours.shape, jnp.int32)] * 3

    (edges,) = call(
        functools.partial(pack_kernel, length=length), "pack_edges", "h", [shape((block, size, chans), BF)],
        [scratch(x.shape, BF), scratch((count, chans), F32)], patches, small=(0,), room=ROOM,
    )(x)
    from_low = shifted(edges, 2)
    from_high = shifted(edges, -2)
    from_mate = swapped(edges, 1)

    own, far, near, dw, dx, mid = own_pixels(tables, x, cot, w, bias_vector.reshape(1, chans), flips, devices)
    dx, mid = dx.reshape(x.shape), mid.reshape(x.shape)
    near_in = swapped(near, 1)

    from_low, from_high, dw = lax.optimization_barrier((from_low, from_high, dw))
    from_across = swapped(jnp.where(core == 0, from_high, from_low), 1)

    cross_terms = near_in[block:].astype(F32)
    to_low = (far[:block] + jnp.where(core == 1, cross_terms, 0.0)).astype(BF)
    to_high = (far[block:] + jnp.where(core == 0, cross_terms, 0.0)).astype(BF)

    factor = 1.0 / (length * math.sqrt(patches * devices))
    keep, send, halo = call(
        functools.partial(halo_kernel, length=length, devices=devices, factor=factor), "halo_kernel_grad",
        "shhhvvvvvahh",
        [
            shape((rows // 2, chans), F32),
            shape((rows // 2, chans), F32),
            shape((4, patches * size, 3 * chans), BF),
        ],
        table_scratch
        + [
            scratch((5 * block, size, chans), BF),
            scratch(dw.shape, F32),
            scratch(sides.shape, BF),
            scratch(ends.shape, BF),
            scratch((4, patches * size, 3 * chans), BF),
        ],
        7, small=(0, 1), room=ROOM,
    )(*tables, edges, from_low, from_high, from_mate, from_across, dw, sides, ends)

    (outputs,) = call(
        functools.partial(forward_kernel, length=length), "add_halo_outputs", "aha", [shape(x.shape, BF)],
        [scratch(x.shape, F32), scratch(w.shape, BF), scratch(halo.shape, BF), scratch(x.shape, BF)], 2 + 2 * patches, room=ROOM,
    )(mid, w, halo)

    terms_high = shifted(to_low, -2)
    terms_low = shifted(to_high, 2)
    results = {}

    def between(value):
        value, results["high"], results["low"], results["out"] = lax.optimization_barrier(
            (value, terms_high, terms_low, outputs)
        )
        return value

    def last(value):
        (input_grad,) = call(
            functools.partial(join_kernel, length=length), "join_input_grad", "aavvv", [shape(x.shape, BF)],
            [
                scratch(x.shape, BF),
                scratch((block, size, chans), F32),
                scratch(x.shape, BF),
                scratch((count, chans), F32),
            ],
            1 + 2 * patches, room=ROOM,
        )(dx, own, near_in, results["low"], results["high"])
        value, results["in"] = lax.optimization_barrier((value, input_grad))
        return value

    mine, other = summed(keep, send, me, devices, between, last)
    grad_shapes = [shape((9 * chans, chans), F32), shape((1, chans), F32)]
    weight_grad, bias_grad = call(
        functools.partial(half_kernel, mates=False), "place_own_half", "sv", grad_shapes, [], 1, small=(1,), room=ROOM,
    )(me_arr, mine)
    (weight_grad,) = call(
        functools.partial(half_kernel, mates=True), "place_mates_half", "sva", grad_shapes[:1], [], 1, room=ROOM,
        aliases={2: 0},
    )(me_arr, other, weight_grad)
    return (
        results["out"].reshape(inputs.shape),
        results["in"].reshape(inputs.shape),
        weight_grad.reshape(weights.shape),
        bias_grad.reshape(bias_vector.shape),
    )


def solution(mesh):
    in_specs = (
        P("patch", None, None, None),
        P("patch", None, None, None),
        P(),
        P(),
        P("patch", None),
        P("patch", None),
        P("patch", None),
    )
    out_specs = (P("patch", None, None, None), P("patch", None, None, None), P(), P())
    return jax.shard_map(body, mesh=mesh, in_specs=in_specs, out_specs=out_specs, check_vma=False)
```

```python
import functools
import math

import jax
import jax.numpy as jnp
import numpy as np
from jax import lax
from jax.experimental import pallas as pl
from jax.experimental.pallas import tpu as pltpu
from jax.sharding import PartitionSpec as P

ROOM = 12
STEP = 4
BF = jnp.bfloat16
F32 = jnp.float32

DIRECTIONS = ((-1, -1), (-1, 0), (-1, 1), (0, -1), (0, 1), (1, -1), (1, 0), (1, 1))
SIDE_TABLE = (
    ((0, 0), (3, 1), (1, 3), (2, 2)),
    ((1, 0), (2, 1), (0, 3), (3, 2)),
    ((2, 0), (0, 2), (3, 3), (1, 1)),
    ((3, 0), (1, 2), (2, 3), (0, 1)),
)
SIDE_DIRECTION = (1, 6, 3, 4)
SIDE_ENDS = ((0, 2), (5, 7))
SIDE_TAPS = (((0, 0), (0, 1), (0, 2)), ((2, 0), (2, 1), (2, 2)), ((0, 0), (1, 0), (2, 0)), ((0, 2), (1, 2), (2, 2)))


def wanted_side(row_step, col_step):
    if row_step < 0:
        return 1
    if row_step > 0:
        return 0
    return 3 if col_step < 0 else 2


def flip_tables(length):
    size = 2 * length
    flips = np.zeros((4, size, size), np.float32)
    for code in range(4):
        for r in range(2):
            for k in range(length):
                rr = 1 - r if code & 1 else r
                kk = length - 1 - k if code & 2 else k
                flips[code, r * length + k, rr * length + kk] = 1
    back = np.zeros((2, size, size), np.float32)
    ahead = np.zeros((2, size, size), np.float32)
    for r in range(2):
        for k in range(length):
            back[int(k < 2), r * length + k, r * length + (k - 2) % length] = 1
            ahead[int(k >= length - 2), r * length + k, r * length + (k + 2) % length] = 1
    sides = np.stack([np.concatenate([back[0] @ f, f, ahead[0] @ f]) for f in flips])
    ends = np.stack([np.concatenate([back[1] @ f, ahead[1] @ f]) for f in flips])
    return flips, sides, ends


def place_of(me, neighbour, rotation, which, patches_here, devices):
    owner = lax.div(neighbour, patches_here)
    within = neighbour - owner * patches_here
    offset = owner - me
    offset = jnp.where(offset < 0, offset + devices, offset)
    core = lax.rem(me, 2)
    to_mate = jnp.where(core == 0, 1, devices - 1)
    block = jnp.where(offset == to_mate, 3, 4)
    block = jnp.where(offset == 2, 2, block)
    block = jnp.where(offset == devices - 2, 1, block)
    block = jnp.where(offset == 0, 0, block)
    slot, code = SIDE_TABLE[which][0]
    for k in range(1, 4):
        slot = jnp.where(rotation == k, SIDE_TABLE[which][k][0], slot)
        code = jnp.where(rotation == k, SIDE_TABLE[which][k][1], code)
    return (block * patches_here + within) * 4 + slot, code


def dot(a, b):
    return jnp.dot(a, b, preferred_element_type=F32)


def column_strip(wide_ref, first, length):
    return jnp.concatenate([wide_ref[pl.ds(first + c, length, stride=length), :] for c in range(2)], axis=0)


def add_columns(wide_ref, first, length, strip):
    for c in range(2):
        at = pl.ds(first + c, length, stride=length)
        wide_ref[at, :] = wide_ref[at, :] + strip[c * length : (c + 1) * length]


def spread(ext_ref, wide, length):
    count = length * length
    size = 2 * length
    column = lax.broadcasted_iota(jnp.int32, (count, 1), 0) & (length - 1)
    back = jnp.where(column >= 2, pltpu.roll(wide, 2, 0), 0.0)
    ahead = jnp.where(column < length - 2, pltpu.roll(wide, count - 2, 0), 0.0)
    for i, part in enumerate((back, wide, ahead)):
        part = part.astype(BF)
        lanes = slice(i * 128, (i + 1) * 128)
        groups = count // (2 * size)
        for g in range(groups):
            at = 2 * size * g
            ext_ref[g, size:, lanes] = part[at : at + size]
            ext_ref[g + 1, 0:size, lanes] = part[at + size : at + 2 * size]


def clear_rows(ext_ref, length):
    size = 2 * length
    empty = jnp.zeros((size, 384), BF)
    ext_ref[0, 0:size, :] = empty
    ext_ref[ext_ref.shape[0] - 1, size:, :] = empty


def pair_taps(rows_of):
    none = jnp.zeros_like(rows_of[0])
    left = rows_of + [none]
    right = [none] + rows_of
    both = [jnp.concatenate([a, b], axis=1) for a, b in zip(left, right)]
    return [jnp.concatenate(both[0:2], axis=0), jnp.concatenate(both[2:4], axis=0)]


def conv_pairs(ext_ref, weights, first, groups, length):
    size = 2 * length
    total = None
    for half in range(2):
        rows = ext_ref[first + half : first + half + groups]
        pixels = jnp.concatenate(
            [rows[:, 0:size].reshape(groups * size, 384), rows[:, size:].reshape(groups * size, 384)], axis=1
        )
        part = dot(pixels, weights[half])
        total = part if total is None else total + part
    return total[:, 0:128].reshape(groups, size, 128), total[:, 128:].reshape(groups, size, 128)


def begin(source, target, sem):
    copy = pltpu.make_async_copy(source, target, sem)
    copy.start()
    return copy


def finish(copies):
    for copy in copies:
        copy.wait()


def pack_kernel(x_ref, out_vm, x_vm, wide_ref, sems, *, length):
    count = length * length
    patches = x_vm.shape[0]
    arriving = [begin(x_ref.at[p], x_vm.at[p], sems.at[p]) for p in range(patches)]
    for p in range(patches):
        arriving[p].wait()
        out_vm[4 * p] = x_vm[p, 0 : 2 * length, :]
        out_vm[4 * p + 1] = x_vm[p, count - 2 * length :, :]
        wide_ref[...] = x_vm[p].astype(F32)
        out_vm[4 * p + 2] = column_strip(wide_ref, 0, length).astype(BF)
        out_vm[4 * p + 3] = column_strip(wide_ref, length - 2, length).astype(BF)


def own_kernel(
    me_ref, nb_ref, rot_ref, cor_ref, x_ref, cot_ref, w_ref, bias_in_ref, flip_ref,
    own_ref, far_ref, near_ref, dw_ref, dx_ref, mid_ref,
    nb_sm, rot_sm, cor_sm, x_vm, cot_vm, w_vm, bias_in_vm, flip_vm,
    strips_vm, near_vm, dw_vm, dx_vm, mid_vm, ext_ref, wide_ref, pool_ref, sems, *, length, devices,
):
    patches = x_vm.shape[0]
    count = length * length
    size = 2 * length
    block = 4 * patches
    sources = [nb_ref, rot_ref, cor_ref, w_ref, bias_in_ref, flip_ref]
    targets = [nb_sm, rot_sm, cor_sm, w_vm, bias_in_vm, flip_vm]
    arriving = [begin(a, b, sems.at[i]) for i, (a, b) in enumerate(zip(sources, targets))]
    used = len(arriving)
    cots = [begin(cot_ref.at[p], cot_vm.at[p], sems.at[used + p]) for p in range(patches)]
    used += patches
    xs = [begin(x_ref.at[p], x_vm.at[p], sems.at[used + p]) for p in range(patches)]
    used += patches
    leaving = []
    me = me_ref[0]
    pool_ref[...] = jnp.zeros_like(pool_ref)
    clear_rows(ext_ref, length)
    along = lax.broadcasted_iota(jnp.int32, (length, 1), 0)
    finish(arriving)
    taps = [jnp.concatenate([w_vm[a * 3 + b] for a, b in SIDE_TAPS[s]], axis=0) for s in range(4)]
    for p in range(patches):
        cots[p].wait()
        mine = slice(size * p, size * (p + 1))
        strips_vm[0, mine, :] = cot_vm[p, 0:size, :]
        strips_vm[1, mine, :] = cot_vm[p, count - size :, :]
        wide_ref[...] = cot_vm[p].astype(F32)
        strips_vm[2, mine, :] = column_strip(wide_ref, 0, length).astype(BF)
        strips_vm[3, mine, :] = column_strip(wide_ref, length - 2, length).astype(BF)
    sent = []
    for s in range(4):
        terms = lax.dot_general(strips_vm[s], taps[s], (((1,), (1,)), ((), ())), preferred_element_type=F32)
        for p in range(patches):
            side, first, last = [], [], []
            for r in range(2):
                rows = slice(size * p + r * length, size * p + (r + 1) * length)
                ahead = pltpu.roll(terms[rows, 0:128], length - 2, 0)
                back = pltpu.roll(terms[rows, 256:384], 2, 0)
                side.append(
                    terms[rows, 128:256]
                    + jnp.where(along < length - 2, ahead, 0.0)
                    + jnp.where(along >= 2, back, 0.0)
                )
                first.append(jnp.where(along >= length - 2, ahead, 0.0))
                last.append(jnp.where(along < 2, back, 0.0))
            sent.append((p, SIDE_DIRECTION[s], side))
            if s < 2:
                sent += [(p, SIDE_ENDS[s][0], first), (p, SIDE_ENDS[s][1], last)]
    placed = []
    for p, j, term in sent:
        where_to, code = place_of(me, nb_sm[p, j], rot_sm[p, j], wanted_side(*DIRECTIONS[j]), patches, devices)
        value = dot(flip_vm[code], jnp.concatenate(term, axis=0).astype(BF))
        placed.append((where_to, value * (cor_sm[p, j] > 0).astype(F32)))
    for where_to, value in placed:
        pool_ref[where_to] = pool_ref[where_to] + value
    near_vm[...] = pool_ref[3 * block :].astype(BF)
    for source, target in (
        (near_vm, near_ref),
        (pool_ref.at[pl.ds(0, block)], own_ref), (pool_ref.at[pl.ds(block, 2 * block)], far_ref),
    ):
        leaving.append(begin(source, target, sems.at[used]))
        used += 1

    total_bias = jnp.zeros((1, 128), F32)
    flipped = pair_taps(
        [jnp.concatenate([w_vm[(2 - a) * 3 + 2 - b].T for b in range(3)], axis=0) for a in range(3)]
    )
    plain = pair_taps([jnp.concatenate([w_vm[a * 3 + b] for b in range(3)], axis=0) for a in range(3)])
    groups = count // (2 * size)
    step = min(groups, STEP)
    for p in range(patches):
        wide = cot_vm[p].astype(F32)
        total_bias = total_bias + jnp.sum(wide, axis=0, keepdims=True)
        spread(ext_ref, wide, length)
        xs[p].wait()
        turned = x_vm[p].T
        windows = [
            ext_ref[0:groups].reshape(count, 384),
            jnp.concatenate([ext_ref[0:groups, size:], ext_ref[1 : groups + 1, 0:size]], axis=1).reshape(count, 384),
            ext_ref[1 : groups + 1].reshape(count, 384),
        ]
        for a in range(3):
            grads = dot(turned, windows[a])
            for b in range(3):
                tap = (2 - a) * 3 + 2 - b
                rows = slice(tap * 128, (tap + 1) * 128)
                part = grads[:, b * 128 : (b + 1) * 128]
                dw_vm[rows, :] = part if p == 0 else dw_vm[rows, :] + part
        for g in range(0, groups, step):
            for i, part in enumerate(conv_pairs(ext_ref, flipped, g, step, length)):
                dx_vm[p, g : g + step, i * size : (i + 1) * size] = part.astype(BF)
        leaving.append(begin(dx_vm.at[p], dx_ref.at[p], sems.at[used]))
        used += 1
    dw_vm[9 * 128 : 10 * 128, :] = jnp.zeros((128, 128), F32)
    dw_vm[9 * 128 : 9 * 128 + 8, :] = jnp.broadcast_to(total_bias, (8, 128))
    for s in range(4):
        at = 10 * 128 + s * patches * size
        dw_vm[at : at + patches * size, :] = strips_vm[s].astype(F32)
    leaving.append(begin(dw_vm, dw_ref, sems.at[used]))
    used += 1
    for p in range(patches):
        spread(ext_ref, x_vm[p].astype(F32), length)
        for g in range(0, groups, step):
            for i, part in enumerate(conv_pairs(ext_ref, plain, g, step, length)):
                mid_vm[p, g : g + step, i * size : (i + 1) * size] = part + bias_in_vm[...]
        leaving.append(begin(mid_vm.at[p], mid_ref.at[p], sems.at[used]))
        used += 1
    finish(leaving)


def halo_kernel(
    me_ref, nb_ref, rot_ref, cor_ref, own_ref, low_ref, high_ref, mate_ref, across_ref, dw_ref,
    side_vm, end_vm, keep_ref, send_ref, halo_ref,
    nb_sm, rot_sm, cor_sm, pool_ref, total_ref, halo_vm, sems, *, length, devices, factor,
):
    block = pool_ref.shape[0] // 5
    patches = block // 4
    sources = [nb_ref, rot_ref, cor_ref]
    targets = [nb_sm, rot_sm, cor_sm]
    arriving = [begin(a, b, sems.at[i]) for i, (a, b) in enumerate(zip(sources, targets))]
    used = len(arriving)
    later = [begin(dw_ref, total_ref, sems.at[used])]
    used += 1
    for i, source in enumerate((own_ref, low_ref, high_ref, mate_ref, across_ref)):
        pool_ref[i * block : (i + 1) * block] = source[...]
    me = me_ref[0]
    size = 2 * length
    finish(arriving)
    for p in range(patches):

        def fetch(j):
            at, code = place_of(me, nb_sm[p, j], rot_sm[p, j], wanted_side(*DIRECTIONS[j]), patches, devices)
            return pool_ref[at], code

        for s in range(4):
            source, code = fetch(SIDE_DIRECTION[s])
            shifted = dot(side_vm[code], source)
            parts = [shifted[0:size], shifted[size : 2 * size], shifted[2 * size :]]
            if s < 2:
                for which, j in ((0, SIDE_ENDS[s][0]), (1, SIDE_ENDS[s][1])):
                    source, code = fetch(j)
                    corner = dot(end_vm[code, which * size : (which + 1) * size, :], source)
                    parts[2 * which] = parts[2 * which] + corner * (cor_sm[p, j] > 0).astype(F32)
            for i in range(3):
                halo_vm[s, p * size : (p + 1) * size, i * 128 : (i + 1) * 128] = parts[i].astype(BF)
    leaving = [begin(halo_vm, halo_ref, sems.at[used])]
    finish(later)
    for s in range(4):
        at = 10 * 128 + s * patches * size
        strips = total_ref[at : at + patches * size, :].astype(BF)
        grads = lax.dot_general(
            halo_vm[s], strips, (((0,), (0,)), ((), ())), preferred_element_type=F32
        )
        for i, (a, b) in enumerate(SIDE_TAPS[s]):
            rows = slice((a * 3 + b) * 128, (a * 3 + b + 1) * 128)
            total_ref[rows, :] = total_ref[rows, :] + grads[i * 128 : (i + 1) * 128]
    taps = 9 * 128
    half = taps // 2
    core = lax.rem(me, 2)
    for target, which in ((send_ref, 1 - core), (keep_ref, core)):
        target[0:half, :] = total_ref[pl.ds(pl.multiple_of(which * half, 64), half), :] * factor
        target[half:, :] = total_ref[taps : taps + target.shape[0] - half, :] * factor
    finish(leaving)


def forward_kernel(mid_ref, w_ref, halo_ref, out_ref, mid_vm, w_vm, halo_vm, out_vm, sems, *, length):
    count = length * length
    size = 2 * length
    patches = mid_vm.shape[0]
    arriving = [begin(w_ref, w_vm, sems.at[0]), begin(halo_ref, halo_vm, sems.at[1])]
    mids = [begin(mid_ref.at[p], mid_vm.at[p], sems.at[2 + p]) for p in range(patches)]
    finish(arriving)
    borders = []
    for s in range(4):
        taps = jnp.concatenate([w_vm[a * 3 + b] for a, b in SIDE_TAPS[s]], axis=0)
        borders.append(dot(halo_vm[s], taps))
    leaving = []
    for p in range(patches):
        mids[p].wait()
        mine = slice(p * size, (p + 1) * size)
        wide_ref = mid_vm.at[p]
        wide_ref[0:size, :] = wide_ref[0:size, :] + borders[0][mine]
        wide_ref[count - size :, :] = wide_ref[count - size :, :] + borders[1][mine]
        add_columns(wide_ref, 0, length, borders[2][mine])
        add_columns(wide_ref, length - 2, length, borders[3][mine])
        out_vm[p] = wide_ref[...].astype(BF)
        leaving.append(begin(out_vm.at[p], out_ref.at[p], sems.at[2 + patches + p]))
    finish(leaving)


def join_kernel(
    dx_ref, own_ref, near_ref, low_ref, high_ref, out_ref,
    dx_vm, own_vm, out_vm, wide_ref, sems, *, length,
):
    count = length * length
    size = 2 * length
    patches = dx_vm.shape[0]
    arriving = [begin(own_ref, own_vm, sems.at[0])]
    used = len(arriving)
    dxs = [begin(dx_ref.at[p], dx_vm.at[p], sems.at[used + p]) for p in range(patches)]
    used += patches
    finish(arriving)
    leaving = []
    for p in range(patches):
        dxs[p].wait()
        wide_ref[...] = dx_vm[p].astype(F32)
        strips = []
        for s in range(4):
            i = 4 * p + s
            strips.append(own_vm[i] + near_ref[i].astype(F32) + low_ref[i].astype(F32) + high_ref[i].astype(F32))
        wide_ref[0:size, :] = wide_ref[0:size, :] + strips[0]
        wide_ref[count - size :, :] = wide_ref[count - size :, :] + strips[1]
        add_columns(wide_ref, 0, length, strips[2])
        add_columns(wide_ref, length - 2, length, strips[3])
        out_vm[p] = wide_ref[...].astype(BF)
        leaving.append(begin(out_vm.at[p], out_ref.at[p], sems.at[used]))
        used += 1
    finish(leaving)


def half_kernel(me_ref, half_ref, *refs, mates):
    grad_ref, sem = refs[1 if mates else 0], refs[-1]
    half = grad_ref.shape[0] // 2
    core = lax.rem(me_ref[0], 2)
    at = (1 - core) * half if mates else core * half
    copy = begin(half_ref.at[pl.ds(0, half)], grad_ref.at[pl.ds(pl.multiple_of(at, 64), half)], sem.at[0])
    if not mates:
        bias_ref = refs[1]
        bias_ref[...] = half_ref[half : half + 1, :]
    copy.wait()


def call(kernel, name, operands, outs, scratch, copies, small=(), room=4, aliases=None):
    spaces = {"s": pltpu.SMEM, "h": pltpu.HBM, "a": pl.ANY, "v": pltpu.VMEM}
    out_specs = [pl.BlockSpec(memory_space=pltpu.VMEM if i in small else pl.ANY) for i in range(len(outs))]
    return pl.pallas_call(
        kernel,
        name=name,
        out_shape=list(outs),
        input_output_aliases=aliases or {},
        in_specs=[pl.BlockSpec(memory_space=spaces[o]) for o in operands],
        out_specs=out_specs,
        scratch_shapes=list(scratch) + [pltpu.SemaphoreType.DMA((copies,))],
        compiler_params=pltpu.CompilerParams(vmem_limit_bytes=(64 - room) * 1024 * 1024),
        cost_estimate=pl.CostEstimate(flops=0, bytes_accessed=0, transcendentals=0),
    )


def shifted(value, steps):
    count = lax.axis_size("patch")
    return lax.ppermute(value, "patch", [(d, (d + steps) % count) for d in range(count)])


def swapped(value, mask):
    return lax.ppermute(value, "patch", [(d, d ^ mask) for d in range(lax.axis_size("patch"))])


def part_of(value, index, size):
    return lax.dynamic_slice_in_dim(value, index * size, size)


def summed(keep, send, me, devices, between, last):
    mine = keep + swapped(send, 1)
    quarter = mine.shape[0] // 4
    at = (me // 2) % 4
    arrived = [swapped(part_of(mine, at ^ k, quarter).astype(BF), 2 * k) for k in (3, 2, 1)]
    mine = part_of(mine, at, quarter)
    for a in arrived:
        mine = mine + a.astype(F32)
    step = 8
    while step < devices:
        sent = mine.astype(BF)
        arrived = [swapped(sent, k * step) for k in range(1, 4 if 2 * step < devices else 2)]
        if 4 * step >= devices:
            arrived = between(arrived)
        mine = sent.astype(F32) + arrived[0].astype(F32)
        if len(arrived) > 1:
            mine = mine + (arrived[1].astype(F32) + arrived[2].astype(F32))
        step *= 4
    pieces = jnp.stack([mine] + [swapped(mine, 2 * k) for k in range(1, 4)])
    whole = jnp.concatenate([lax.dynamic_index_in_dim(pieces, at ^ k, 0, False) for k in range(4)])
    whole = last(whole)
    return whole, swapped(whole, 1)


def own_pixels(tables, x, cot, w, bias, flips, devices):
    patches, count, chans = x.shape
    length = math.isqrt(count)
    size = 2 * length
    block = 4 * patches
    rows = 10 * chans
    grouped = (patches, count // (2 * size), 2 * size, chans)
    shape = jax.ShapeDtypeStruct
    scratch = pltpu.VMEM
    table_scratch = [pltpu.SMEM(tables[1].shape, jnp.int32)] * 3
    return call(
        functools.partial(own_kernel, length=length, devices=devices), "own_pixels", "shhhhhhhh",
        [
            shape((block, size, chans), F32),
            shape((2 * block, size, chans), F32),
            shape((2 * block, size, chans), BF),
            shape((rows + block * size, chans), F32),
            shape(grouped, BF),
            shape(grouped, F32),
        ],
        table_scratch
        + [
            scratch(x.shape, BF),
            scratch(x.shape, BF),
            scratch(w.shape, BF),
            scratch((1, chans), F32),
            scratch(flips.shape, BF),
            scratch((4, patches * size, chans), BF),
            scratch((2 * block, size, chans), BF),
            scratch((rows + block * size, chans), F32),
            scratch(grouped, BF),
            scratch(grouped, F32),
            scratch((count // (2 * size) + 1, 2 * size, 3 * chans), BF),
            scratch((count, chans), F32),
            scratch((5 * block, size, chans), F32),
        ],
        6 + 4 * patches + 4,
    )(*tables, x, cot, w, bias, flips)


def body(inputs, cotangent, weights, bias_vector, neighbours, rotations, corners):
    patches, length, _, chans = inputs.shape
    devices = lax.axis_size("patch")
    count = length * length
    size = 2 * length
    block = 4 * patches
    rows = 10 * chans
    me = lax.axis_index("patch")
    me_arr = me.reshape(1).astype(jnp.int32)
    core = me % 2
    x = inputs.reshape(patches, count, chans)
    cot = cotangent.reshape(patches, count, chans)
    w = weights.reshape(9, chans, chans)
    flips, sides, ends = (jnp.asarray(t, BF) for t in flip_tables(length))
    shape = jax.ShapeDtypeStruct
    scratch = pltpu.VMEM
    tables = (me_arr, neighbours, rotations, corners)
    table_scratch = [pltpu.SMEM(neighbours.shape, jnp.int32)] * 3

    (edges,) = call(
        functools.partial(pack_kernel, length=length), "pack_edges", "h", [shape((block, size, chans), BF)],
        [scratch(x.shape, BF), scratch((count, chans), F32)], patches, small=(0,), room=ROOM,
    )(x)
    from_low = shifted(edges, 2)
    from_high = shifted(edges, -2)
    from_mate = swapped(edges, 1)

    own, far, near, dw, dx, mid = own_pixels(tables, x, cot, w, bias_vector.reshape(1, chans), flips, devices)
    dx, mid = dx.reshape(x.shape), mid.reshape(x.shape)
    near_in = swapped(near, 1)

    from_low, from_high, dw = lax.optimization_barrier((from_low, from_high, dw))
    from_across = swapped(jnp.where(core == 0, from_high, from_low), 1)

    cross_terms = near_in[block:].astype(F32)
    to_low = (far[:block] + jnp.where(core == 1, cross_terms, 0.0)).astype(BF)
    to_high = (far[block:] + jnp.where(core == 0, cross_terms, 0.0)).astype(BF)

    factor = 1.0 / (length * math.sqrt(patches * devices))
    keep, send, halo = call(
        functools.partial(halo_kernel, length=length, devices=devices, factor=factor), "halo_kernel_grad",
        "shhhvvvvvavv",
        [
            shape((rows // 2, chans), F32),
            shape((rows // 2, chans), F32),
            shape((4, patches * size, 3 * chans), BF),
        ],
        table_scratch
        + [
            scratch((5 * block, size, chans), BF),
            scratch(dw.shape, F32),
            scratch((4, patches * size, 3 * chans), BF),
        ],
        5, small=(0, 1), room=ROOM,
    )(*tables, edges, from_low, from_high, from_mate, from_across, dw, sides, ends)

    (outputs,) = call(
        functools.partial(forward_kernel, length=length), "add_halo_outputs", "aha", [shape(x.shape, BF)],
        [scratch(x.shape, F32), scratch(w.shape, BF), scratch(halo.shape, BF), scratch(x.shape, BF)], 2 + 2 * patches, room=ROOM,
    )(mid, w, halo)

    terms_high = shifted(to_low, -2)
    terms_low = shifted(to_high, 2)
    results = {}

    def between(value):
        value, results["low"], results["out"] = lax.optimization_barrier((value, terms_low, outputs))
        results["high"] = terms_high
        return value

    def last(value):
        (input_grad,) = call(
            functools.partial(join_kernel, length=length), "join_input_grad", "aavvv", [shape(x.shape, BF)],
            [
                scratch(x.shape, BF),
                scratch((block, size, chans), F32),
                scratch(x.shape, BF),
                scratch((count, chans), F32),
            ],
            1 + 2 * patches, room=ROOM,
        )(dx, own, near_in, results["low"], results["high"])
        value, results["in"] = lax.optimization_barrier((value, input_grad))
        return value

    mine, other = summed(keep, send, me, devices, between, last)
    grad_shapes = [shape((9 * chans, chans), F32), shape((1, chans), F32)]
    weight_grad, bias_grad = call(
        functools.partial(half_kernel, mates=False), "place_own_half", "sv", grad_shapes, [], 1, small=(1,), room=ROOM,
    )(me_arr, mine)
    (weight_grad,) = call(
        functools.partial(half_kernel, mates=True), "place_mates_half", "sva", grad_shapes[:1], [], 1, room=ROOM,
        aliases={2: 0},
    )(me_arr, other, weight_grad)
    return (
        results["out"].reshape(inputs.shape),
        results["in"].reshape(inputs.shape),
        weight_grad.reshape(weights.shape),
        bias_grad.reshape(bias_vector.shape),
    )


def solution(mesh):
    in_specs = (
        P("patch", None, None, None),
        P("patch", None, None, None),
        P(),
        P(),
        P("patch", None),
        P("patch", None),
        P("patch", None),
    )
    out_specs = (P("patch", None, None, None), P("patch", None, None, None), P(), P())
    return jax.shard_map(body, mesh=mesh, in_specs=in_specs, out_specs=out_specs, check_vma=False)
```

```python
import functools
import math

import jax
import jax.numpy as jnp
import numpy as np
from jax import lax
from jax.experimental import pallas as pl
from jax.experimental.pallas import tpu as pltpu
from jax.sharding import PartitionSpec as P

ROOM = 12
STEP = 4
BF = jnp.bfloat16
F32 = jnp.float32

DIRECTIONS = ((-1, -1), (-1, 0), (-1, 1), (0, -1), (0, 1), (1, -1), (1, 0), (1, 1))
SIDE_TABLE = (
    ((0, 0), (3, 1), (1, 3), (2, 2)),
    ((1, 0), (2, 1), (0, 3), (3, 2)),
    ((2, 0), (0, 2), (3, 3), (1, 1)),
    ((3, 0), (1, 2), (2, 3), (0, 1)),
)
SIDE_DIRECTION = (1, 6, 3, 4)
SIDE_ENDS = ((0, 2), (5, 7))
SIDE_TAPS = (((0, 0), (0, 1), (0, 2)), ((2, 0), (2, 1), (2, 2)), ((0, 0), (1, 0), (2, 0)), ((0, 2), (1, 2), (2, 2)))


def wanted_side(row_step, col_step):
    if row_step < 0:
        return 1
    if row_step > 0:
        return 0
    return 3 if col_step < 0 else 2


def flip_tables(length):
    size = 2 * length
    flips = np.zeros((4, size, size), np.float32)
    for code in range(4):
        for r in range(2):
            for k in range(length):
                rr = 1 - r if code & 1 else r
                kk = length - 1 - k if code & 2 else k
                flips[code, r * length + k, rr * length + kk] = 1
    back = np.zeros((2, size, size), np.float32)
    ahead = np.zeros((2, size, size), np.float32)
    for r in range(2):
        for k in range(length):
            back[int(k < 2), r * length + k, r * length + (k - 2) % length] = 1
            ahead[int(k >= length - 2), r * length + k, r * length + (k + 2) % length] = 1
    sides = np.stack([np.concatenate([back[0] @ f, f, ahead[0] @ f]) for f in flips])
    ends = np.stack([np.concatenate([back[1] @ f, ahead[1] @ f]) for f in flips])
    return flips, sides, ends


def place_of(me, neighbour, rotation, which, patches_here, devices):
    owner = lax.div(neighbour, patches_here)
    within = neighbour - owner * patches_here
    offset = owner - me
    offset = jnp.where(offset < 0, offset + devices, offset)
    core = lax.rem(me, 2)
    to_mate = jnp.where(core == 0, 1, devices - 1)
    block = jnp.where(offset == to_mate, 3, 4)
    block = jnp.where(offset == 2, 2, block)
    block = jnp.where(offset == devices - 2, 1, block)
    block = jnp.where(offset == 0, 0, block)
    slot, code = SIDE_TABLE[which][0]
    for k in range(1, 4):
        slot = jnp.where(rotation == k, SIDE_TABLE[which][k][0], slot)
        code = jnp.where(rotation == k, SIDE_TABLE[which][k][1], code)
    return (block * patches_here + within) * 4 + slot, code


def dot(a, b):
    return jnp.dot(a, b, preferred_element_type=F32)


def column_strip(wide_ref, first, length):
    return jnp.concatenate([wide_ref[pl.ds(first + c, length, stride=length), :] for c in range(2)], axis=0)


def add_columns(wide_ref, first, length, strip):
    for c in range(2):
        at = pl.ds(first + c, length, stride=length)
        wide_ref[at, :] = wide_ref[at, :] + strip[c * length : (c + 1) * length]


def spread(ext_ref, wide, length):
    count = length * length
    size = 2 * length
    column = lax.broadcasted_iota(jnp.int32, (count, 1), 0) & (length - 1)
    back = jnp.where(column >= 2, pltpu.roll(wide, 2, 0), 0.0)
    ahead = jnp.where(column < length - 2, pltpu.roll(wide, count - 2, 0), 0.0)
    for i, part in enumerate((back, wide, ahead)):
        part = part.astype(BF)
        lanes = slice(i * 128, (i + 1) * 128)
        groups = count // (2 * size)
        for g in range(groups):
            at = 2 * size * g
            ext_ref[g, size:, lanes] = part[at : at + size]
            ext_ref[g + 1, 0:size, lanes] = part[at + size : at + 2 * size]


def clear_rows(ext_ref, length):
    size = 2 * length
    empty = jnp.zeros((size, 384), BF)
    ext_ref[0, 0:size, :] = empty
    ext_ref[ext_ref.shape[0] - 1, size:, :] = empty


def pair_taps(rows_of):
    none = jnp.zeros_like(rows_of[0])
    left = rows_of + [none]
    right = [none] + rows_of
    both = [jnp.concatenate([a, b], axis=1) for a, b in zip(left, right)]
    return [jnp.concatenate(both[0:2], axis=0), jnp.concatenate(both[2:4], axis=0)]


def conv_pairs(ext_ref, weights, first, groups, length):
    size = 2 * length
    total = None
    for half in range(2):
        rows = ext_ref[first + half : first + half + groups]
        pixels = jnp.concatenate(
            [rows[:, 0:size].reshape(groups * size, 384), rows[:, size:].reshape(groups * size, 384)], axis=1
        )
        part = dot(pixels, weights[half])
        total = part if total is None else total + part
    return total[:, 0:128].reshape(groups, size, 128), total[:, 128:].reshape(groups, size, 128)


def begin(source, target, sem):
    copy = pltpu.make_async_copy(source, target, sem)
    copy.start()
    return copy


def finish(copies):
    for copy in copies:
        copy.wait()


def pack_kernel(x_ref, out_vm, x_vm, wide_ref, sems, *, length):
    count = length * length
    patches = x_vm.shape[0]
    arriving = [begin(x_ref.at[p], x_vm.at[p], sems.at[p]) for p in range(patches)]
    for p in range(patches):
        arriving[p].wait()
        out_vm[4 * p] = x_vm[p, 0 : 2 * length, :]
        out_vm[4 * p + 1] = x_vm[p, count - 2 * length :, :]
        wide_ref[...] = x_vm[p].astype(F32)
        out_vm[4 * p + 2] = column_strip(wide_ref, 0, length).astype(BF)
        out_vm[4 * p + 3] = column_strip(wide_ref, length - 2, length).astype(BF)


def own_kernel(
    me_ref, nb_ref, rot_ref, cor_ref, x_ref, cot_ref, w_ref, bias_in_ref, flip_ref,
    own_ref, far_ref, near_ref, dw_ref, dx_ref, mid_ref,
    nb_sm, rot_sm, cor_sm, x_vm, cot_vm, w_vm, bias_in_vm, flip_vm,
    strips_vm, near_vm, dw_vm, dx_vm, mid_vm, ext_ref, wide_ref, pool_ref, sems, *, length, devices,
):
    patches = x_vm.shape[0]
    count = length * length
    size = 2 * length
    block = 4 * patches
    sources = [nb_ref, rot_ref, cor_ref, w_ref, bias_in_ref, flip_ref]
    targets = [nb_sm, rot_sm, cor_sm, w_vm, bias_in_vm, flip_vm]
    arriving = [begin(a, b, sems.at[i]) for i, (a, b) in enumerate(zip(sources, targets))]
    used = len(arriving)
    cots = [begin(cot_ref.at[p], cot_vm.at[p], sems.at[used + p]) for p in range(patches)]
    used += patches
    xs = [begin(x_ref.at[p], x_vm.at[p], sems.at[used + p]) for p in range(patches)]
    used += patches
    leaving = []
    me = me_ref[0]
    pool_ref[...] = jnp.zeros_like(pool_ref)
    clear_rows(ext_ref, length)
    along = lax.broadcasted_iota(jnp.int32, (length, 1), 0)
    finish(arriving)
    taps = [jnp.concatenate([w_vm[a * 3 + b] for a, b in SIDE_TAPS[s]], axis=0) for s in range(4)]
    for p in range(patches):
        cots[p].wait()
        mine = slice(size * p, size * (p + 1))
        strips_vm[0, mine, :] = cot_vm[p, 0:size, :]
        strips_vm[1, mine, :] = cot_vm[p, count - size :, :]
        wide_ref[...] = cot_vm[p].astype(F32)
        strips_vm[2, mine, :] = column_strip(wide_ref, 0, length).astype(BF)
        strips_vm[3, mine, :] = column_strip(wide_ref, length - 2, length).astype(BF)
    sent = []
    for s in range(4):
        terms = lax.dot_general(strips_vm[s], taps[s], (((1,), (1,)), ((), ())), preferred_element_type=F32)
        for p in range(patches):
            side, first, last = [], [], []
            for r in range(2):
                rows = slice(size * p + r * length, size * p + (r + 1) * length)
                ahead = pltpu.roll(terms[rows, 0:128], length - 2, 0)
                back = pltpu.roll(terms[rows, 256:384], 2, 0)
                side.append(
                    terms[rows, 128:256]
                    + jnp.where(along < length - 2, ahead, 0.0)
                    + jnp.where(along >= 2, back, 0.0)
                )
                first.append(jnp.where(along >= length - 2, ahead, 0.0))
                last.append(jnp.where(along < 2, back, 0.0))
            sent.append((p, SIDE_DIRECTION[s], side))
            if s < 2:
                sent += [(p, SIDE_ENDS[s][0], first), (p, SIDE_ENDS[s][1], last)]
    placed = []
    for p, j, term in sent:
        where_to, code = place_of(me, nb_sm[p, j], rot_sm[p, j], wanted_side(*DIRECTIONS[j]), patches, devices)
        value = dot(flip_vm[code], jnp.concatenate(term, axis=0).astype(BF))
        placed.append((where_to, value * (cor_sm[p, j] > 0).astype(F32)))
    for where_to, value in placed:
        pool_ref[where_to] = pool_ref[where_to] + value
    near_vm[...] = pool_ref[3 * block :].astype(BF)
    for source, target in (
        (near_vm, near_ref),
        (pool_ref.at[pl.ds(0, block)], own_ref), (pool_ref.at[pl.ds(block, 2 * block)], far_ref),
    ):
        leaving.append(begin(source, target, sems.at[used]))
        used += 1

    total_bias = jnp.zeros((1, 128), F32)
    flipped = pair_taps(
        [jnp.concatenate([w_vm[(2 - a) * 3 + 2 - b].T for b in range(3)], axis=0) for a in range(3)]
    )
    plain = pair_taps([jnp.concatenate([w_vm[a * 3 + b] for b in range(3)], axis=0) for a in range(3)])
    groups = count // (2 * size)
    step = min(groups, STEP)
    for p in range(patches):
        wide = cot_vm[p].astype(F32)
        total_bias = total_bias + jnp.sum(wide, axis=0, keepdims=True)
        spread(ext_ref, wide, length)
        xs[p].wait()
        turned = x_vm[p].T
        windows = [
            ext_ref[0:groups].reshape(count, 384),
            jnp.concatenate([ext_ref[0:groups, size:], ext_ref[1 : groups + 1, 0:size]], axis=1).reshape(count, 384),
            ext_ref[1 : groups + 1].reshape(count, 384),
        ]
        for a in range(3):
            grads = dot(turned, windows[a])
            for b in range(3):
                tap = (2 - a) * 3 + 2 - b
                rows = slice(tap * 128, (tap + 1) * 128)
                part = grads[:, b * 128 : (b + 1) * 128]
                dw_vm[rows, :] = part if p == 0 else dw_vm[rows, :] + part
        for g in range(0, groups, step):
            for i, part in enumerate(conv_pairs(ext_ref, flipped, g, step, length)):
                dx_vm[p, g : g + step, i * size : (i + 1) * size] = part.astype(BF)
        leaving.append(begin(dx_vm.at[p], dx_ref.at[p], sems.at[used]))
        used += 1
    dw_vm[9 * 128 : 10 * 128, :] = jnp.zeros((128, 128), F32)
    dw_vm[9 * 128 : 9 * 128 + 8, :] = jnp.broadcast_to(total_bias, (8, 128))
    for s in range(4):
        at = 10 * 128 + s * patches * size
        dw_vm[at : at + patches * size, :] = strips_vm[s].astype(F32)
    leaving.append(begin(dw_vm, dw_ref, sems.at[used]))
    used += 1
    for p in range(patches):
        spread(ext_ref, x_vm[p].astype(F32), length)
        for g in range(0, groups, step):
            for i, part in enumerate(conv_pairs(ext_ref, plain, g, step, length)):
                mid_vm[p, g : g + step, i * size : (i + 1) * size] = part + bias_in_vm[...]
        leaving.append(begin(mid_vm.at[p], mid_ref.at[p], sems.at[used]))
        used += 1
    finish(leaving)


def halo_kernel(
    me_ref, nb_ref, rot_ref, cor_ref, own_ref, low_ref, high_ref, mate_ref, across_ref, dw_ref,
    side_vm, end_vm, keep_ref, send_ref, halo_ref,
    nb_sm, rot_sm, cor_sm, pool_ref, total_ref, halo_vm, sems, *, length, devices, factor,
):
    block = pool_ref.shape[0] // 5
    patches = block // 4
    sources = [nb_ref, rot_ref, cor_ref]
    targets = [nb_sm, rot_sm, cor_sm]
    arriving = [begin(a, b, sems.at[i]) for i, (a, b) in enumerate(zip(sources, targets))]
    used = len(arriving)
    later = [begin(dw_ref, total_ref, sems.at[used])]
    used += 1
    for i, source in enumerate((own_ref, low_ref, high_ref, mate_ref, across_ref)):
        pool_ref[i * block : (i + 1) * block] = source[...]
    me = me_ref[0]
    size = 2 * length
    finish(arriving)
    for p in range(patches):

        def fetch(j):
            at, code = place_of(me, nb_sm[p, j], rot_sm[p, j], wanted_side(*DIRECTIONS[j]), patches, devices)
            return pool_ref[at], code

        for s in range(4):
            source, code = fetch(SIDE_DIRECTION[s])
            shifted = dot(side_vm[code], source)
            parts = [shifted[0:size], shifted[size : 2 * size], shifted[2 * size :]]
            if s < 2:
                for which, j in ((0, SIDE_ENDS[s][0]), (1, SIDE_ENDS[s][1])):
                    source, code = fetch(j)
                    corner = dot(end_vm[code, which * size : (which + 1) * size, :], source)
                    parts[2 * which] = parts[2 * which] + corner * (cor_sm[p, j] > 0).astype(F32)
            for i in range(3):
                halo_vm[s, p * size : (p + 1) * size, i * 128 : (i + 1) * 128] = parts[i].astype(BF)
    leaving = [begin(halo_vm, halo_ref, sems.at[used])]
    finish(later)
    for s in range(4):
        at = 10 * 128 + s * patches * size
        strips = total_ref[at : at + patches * size, :].astype(BF)
        grads = lax.dot_general(
            halo_vm[s], strips, (((0,), (0,)), ((), ())), preferred_element_type=F32
        )
        for i, (a, b) in enumerate(SIDE_TAPS[s]):
            rows = slice((a * 3 + b) * 128, (a * 3 + b + 1) * 128)
            total_ref[rows, :] = total_ref[rows, :] + grads[i * 128 : (i + 1) * 128]
    taps = 9 * 128
    half = taps // 2
    core = lax.rem(me, 2)
    for target, which in ((send_ref, 1 - core), (keep_ref, core)):
        target[0:half, :] = total_ref[pl.ds(pl.multiple_of(which * half, 64), half), :] * factor
        target[half:, :] = total_ref[taps : taps + target.shape[0] - half, :] * factor
    finish(leaving)


def forward_kernel(mid_ref, w_ref, halo_ref, out_ref, mid_vm, w_vm, halo_vm, out_vm, sems, *, length):
    count = length * length
    size = 2 * length
    patches = mid_vm.shape[0]
    arriving = [begin(w_ref, w_vm, sems.at[0]), begin(halo_ref, halo_vm, sems.at[1])]
    mids = [begin(mid_ref.at[p], mid_vm.at[p], sems.at[2 + p]) for p in range(patches)]
    finish(arriving)
    borders = []
    for s in range(4):
        taps = jnp.concatenate([w_vm[a * 3 + b] for a, b in SIDE_TAPS[s]], axis=0)
        borders.append(dot(halo_vm[s], taps))
    leaving = []
    for p in range(patches):
        mids[p].wait()
        mine = slice(p * size, (p + 1) * size)
        wide_ref = mid_vm.at[p]
        wide_ref[0:size, :] = wide_ref[0:size, :] + borders[0][mine]
        wide_ref[count - size :, :] = wide_ref[count - size :, :] + borders[1][mine]
        add_columns(wide_ref, 0, length, borders[2][mine])
        add_columns(wide_ref, length - 2, length, borders[3][mine])
        out_vm[p] = wide_ref[...].astype(BF)
        leaving.append(begin(out_vm.at[p], out_ref.at[p], sems.at[2 + patches + p]))
    finish(leaving)


def join_kernel(
    dx_ref, own_ref, near_ref, low_ref, high_ref, out_ref,
    dx_vm, own_vm, out_vm, wide_ref, sems, *, length,
):
    count = length * length
    size = 2 * length
    patches = dx_vm.shape[0]
    arriving = [begin(own_ref, own_vm, sems.at[0])]
    used = len(arriving)
    dxs = [begin(dx_ref.at[p], dx_vm.at[p], sems.at[used + p]) for p in range(patches)]
    used += patches
    finish(arriving)
    leaving = []
    for p in range(patches):
        dxs[p].wait()
        wide_ref[...] = dx_vm[p].astype(F32)
        strips = []
        for s in range(4):
            i = 4 * p + s
            strips.append(own_vm[i] + near_ref[i].astype(F32) + low_ref[i].astype(F32) + high_ref[i].astype(F32))
        wide_ref[0:size, :] = wide_ref[0:size, :] + strips[0]
        wide_ref[count - size :, :] = wide_ref[count - size :, :] + strips[1]
        add_columns(wide_ref, 0, length, strips[2])
        add_columns(wide_ref, length - 2, length, strips[3])
        out_vm[p] = wide_ref[...].astype(BF)
        leaving.append(begin(out_vm.at[p], out_ref.at[p], sems.at[used]))
        used += 1
    finish(leaving)


def half_kernel(me_ref, half_ref, *refs, mates):
    grad_ref, sem = refs[1 if mates else 0], refs[-1]
    half = grad_ref.shape[0] // 2
    core = lax.rem(me_ref[0], 2)
    at = (1 - core) * half if mates else core * half
    copy = begin(half_ref.at[pl.ds(0, half)], grad_ref.at[pl.ds(pl.multiple_of(at, 64), half)], sem.at[0])
    if not mates:
        bias_ref = refs[1]
        bias_ref[...] = half_ref[half : half + 1, :]
    copy.wait()


def call(kernel, name, operands, outs, scratch, copies, small=(), room=4, aliases=None):
    spaces = {"s": pltpu.SMEM, "h": pltpu.HBM, "a": pl.ANY, "v": pltpu.VMEM}
    out_specs = [pl.BlockSpec(memory_space=pltpu.VMEM if i in small else pl.ANY) for i in range(len(outs))]
    return pl.pallas_call(
        kernel,
        name=name,
        out_shape=list(outs),
        input_output_aliases=aliases or {},
        in_specs=[pl.BlockSpec(memory_space=spaces[o]) for o in operands],
        out_specs=out_specs,
        scratch_shapes=list(scratch) + [pltpu.SemaphoreType.DMA((copies,))],
        compiler_params=pltpu.CompilerParams(vmem_limit_bytes=(64 - room) * 1024 * 1024),
        cost_estimate=pl.CostEstimate(flops=0, bytes_accessed=0, transcendentals=0),
    )


def shifted(value, steps):
    count = lax.axis_size("patch")
    return lax.ppermute(value, "patch", [(d, (d + steps) % count) for d in range(count)])


def swapped(value, mask):
    return lax.ppermute(value, "patch", [(d, d ^ mask) for d in range(lax.axis_size("patch"))])


def part_of(value, index, size):
    return lax.dynamic_slice_in_dim(value, index * size, size)


def summed(keep, send, me, devices, between, last):
    mine = keep + swapped(send, 1)
    quarter = mine.shape[0] // 4
    at = (me // 2) % 4
    arrived = [swapped(part_of(mine, at ^ k, quarter).astype(BF), 2 * k) for k in (3, 2, 1)]
    mine = part_of(mine, at, quarter)
    for a in arrived:
        mine = mine + a.astype(F32)
    step = 8
    while step < devices:
        sent = mine.astype(BF)
        arrived = [swapped(sent, k * step) for k in range(1, 4 if 2 * step < devices else 2)]
        if 4 * step >= devices:
            arrived = between(arrived)
        mine = sent.astype(F32) + arrived[0].astype(F32)
        if len(arrived) > 1:
            mine = mine + (arrived[1].astype(F32) + arrived[2].astype(F32))
        step *= 4
    pieces = jnp.stack([mine] + [swapped(mine, 2 * k) for k in range(1, 4)])
    whole = jnp.concatenate([lax.dynamic_index_in_dim(pieces, at ^ k, 0, False) for k in range(4)])
    whole = last(whole)
    return whole, swapped(whole, 1)


def own_pixels(tables, x, cot, w, bias, flips, devices):
    patches, count, chans = x.shape
    length = math.isqrt(count)
    size = 2 * length
    block = 4 * patches
    rows = 10 * chans
    grouped = (patches, count // (2 * size), 2 * size, chans)
    shape = jax.ShapeDtypeStruct
    scratch = pltpu.VMEM
    table_scratch = [pltpu.SMEM(tables[1].shape, jnp.int32)] * 3
    return call(
        functools.partial(own_kernel, length=length, devices=devices), "own_pixels", "shhhhhhhh",
        [
            shape((block, size, chans), F32),
            shape((2 * block, size, chans), F32),
            shape((2 * block, size, chans), BF),
            shape((rows + block * size, chans), F32),
            shape(grouped, BF),
            shape(grouped, F32),
        ],
        table_scratch
        + [
            scratch(x.shape, BF),
            scratch(x.shape, BF),
            scratch(w.shape, BF),
            scratch((1, chans), F32),
            scratch(flips.shape, BF),
            scratch((4, patches * size, chans), BF),
            scratch((2 * block, size, chans), BF),
            scratch((rows + block * size, chans), F32),
            scratch(grouped, BF),
            scratch(grouped, F32),
            scratch((count // (2 * size) + 1, 2 * size, 3 * chans), BF),
            scratch((count, chans), F32),
            scratch((5 * block, size, chans), F32),
        ],
        6 + 4 * patches + 4,
    )(*tables, x, cot, w, bias, flips)


def body(inputs, cotangent, weights, bias_vector, neighbours, rotations, corners):
    patches, length, _, chans = inputs.shape
    devices = lax.axis_size("patch")
    count = length * length
    size = 2 * length
    block = 4 * patches
    rows = 10 * chans
    me = lax.axis_index("patch")
    me_arr = me.reshape(1).astype(jnp.int32)
    core = me % 2
    x = inputs.reshape(patches, count, chans)
    cot = cotangent.reshape(patches, count, chans)
    w = weights.reshape(9, chans, chans)
    flips, sides, ends = (jnp.asarray(t, BF) for t in flip_tables(length))
    shape = jax.ShapeDtypeStruct
    scratch = pltpu.VMEM
    tables = (me_arr, neighbours, rotations, corners)
    table_scratch = [pltpu.SMEM(neighbours.shape, jnp.int32)] * 3

    (edges,) = call(
        functools.partial(pack_kernel, length=length), "pack_edges", "h", [shape((block, size, chans), BF)],
        [scratch(x.shape, BF), scratch((count, chans), F32)], patches, small=(0,), room=ROOM,
    )(x)
    from_low = shifted(edges, 2)
    from_high = shifted(edges, -2)
    from_mate = swapped(edges, 1)

    own, far, near, dw, dx, mid = own_pixels(tables, x, cot, w, bias_vector.reshape(1, chans), flips, devices)
    dx, mid = dx.reshape(x.shape), mid.reshape(x.shape)
    near_in = swapped(near, 1)

    from_low, from_high, dw = lax.optimization_barrier((from_low, from_high, dw))
    from_across = swapped(jnp.where(core == 0, from_high, from_low), 1)

    cross_terms = near_in[block:].astype(F32)
    to_low = (far[:block] + jnp.where(core == 1, cross_terms, 0.0)).astype(BF)
    to_high = (far[block:] + jnp.where(core == 0, cross_terms, 0.0)).astype(BF)

    factor = 1.0 / (length * math.sqrt(patches * devices))
    keep, send, halo = call(
        functools.partial(halo_kernel, length=length, devices=devices, factor=factor), "halo_kernel_grad",
        "shhhvvvvvavv",
        [
            shape((rows // 2, chans), F32),
            shape((rows // 2, chans), F32),
            shape((4, patches * size, 3 * chans), BF),
        ],
        table_scratch
        + [
            scratch((5 * block, size, chans), BF),
            scratch(dw.shape, F32),
            scratch((4, patches * size, 3 * chans), BF),
        ],
        5, small=(0, 1), room=ROOM,
    )(*tables, edges, from_low, from_high, from_mate, from_across, dw, sides, ends)

    (outputs,) = call(
        functools.partial(forward_kernel, length=length), "add_halo_outputs", "aha", [shape(x.shape, BF)],
        [scratch(x.shape, F32), scratch(w.shape, BF), scratch(halo.shape, BF), scratch(x.shape, BF)], 2 + 2 * patches, room=ROOM,
    )(mid, w, halo)

    terms_high = shifted(to_low, -2)
    terms_low = shifted(to_high, 2)
    results = {}

    def between(value):
        value, results["low"] = lax.optimization_barrier((value, terms_low))
        results["high"] = terms_high
        return value

    def last(value):
        (input_grad,) = call(
            functools.partial(join_kernel, length=length), "join_input_grad", "aavvv", [shape(x.shape, BF)],
            [
                scratch(x.shape, BF),
                scratch((block, size, chans), F32),
                scratch(x.shape, BF),
                scratch((count, chans), F32),
            ],
            1 + 2 * patches, room=ROOM,
        )(dx, own, near_in, results["low"], results["high"])
        value, results["in"], results["out"] = lax.optimization_barrier((value, input_grad, outputs))
        return value

    mine, other = summed(keep, send, me, devices, between, last)
    grad_shapes = [shape((9 * chans, chans), F32), shape((1, chans), F32)]
    weight_grad, bias_grad = call(
        functools.partial(half_kernel, mates=False), "place_own_half", "sv", grad_shapes, [], 1, small=(1,), room=ROOM,
    )(me_arr, mine)
    (weight_grad,) = call(
        functools.partial(half_kernel, mates=True), "place_mates_half", "sva", grad_shapes[:1], [], 1, room=ROOM,
        aliases={2: 0},
    )(me_arr, other, weight_grad)
    return (
        results["out"].reshape(inputs.shape),
        results["in"].reshape(inputs.shape),
        weight_grad.reshape(weights.shape),
        bias_grad.reshape(bias_vector.shape),
    )


def solution(mesh):
    in_specs = (
        P("patch", None, None, None),
        P("patch", None, None, None),
        P(),
        P(),
        P("patch", None),
        P("patch", None),
        P("patch", None),
    )
    out_specs = (P("patch", None, None, None), P("patch", None, None, None), P(), P())
    return jax.shard_map(body, mesh=mesh, in_specs=in_specs, out_specs=out_specs, check_vma=False)
```

```python
import functools
import math

import jax
import jax.numpy as jnp
import numpy as np
from jax import lax
from jax.experimental import pallas as pl
from jax.experimental.pallas import tpu as pltpu
from jax.sharding import PartitionSpec as P

ROOM = 12
STEP = 4
BF = jnp.bfloat16
F32 = jnp.float32

DIRECTIONS = ((-1, -1), (-1, 0), (-1, 1), (0, -1), (0, 1), (1, -1), (1, 0), (1, 1))
SIDE_TABLE = (
    ((0, 0), (3, 1), (1, 3), (2, 2)),
    ((1, 0), (2, 1), (0, 3), (3, 2)),
    ((2, 0), (0, 2), (3, 3), (1, 1)),
    ((3, 0), (1, 2), (2, 3), (0, 1)),
)
SIDE_DIRECTION = (1, 6, 3, 4)
SIDE_ENDS = ((0, 2), (5, 7))
SIDE_TAPS = (((0, 0), (0, 1), (0, 2)), ((2, 0), (2, 1), (2, 2)), ((0, 0), (1, 0), (2, 0)), ((0, 2), (1, 2), (2, 2)))


def wanted_side(row_step, col_step):
    if row_step < 0:
        return 1
    if row_step > 0:
        return 0
    return 3 if col_step < 0 else 2


def flip_tables(length):
    size = 2 * length
    flips = np.zeros((4, size, size), np.float32)
    for code in range(4):
        for r in range(2):
            for k in range(length):
                rr = 1 - r if code & 1 else r
                kk = length - 1 - k if code & 2 else k
                flips[code, r * length + k, rr * length + kk] = 1
    back = np.zeros((2, size, size), np.float32)
    ahead = np.zeros((2, size, size), np.float32)
    for r in range(2):
        for k in range(length):
            back[int(k < 2), r * length + k, r * length + (k - 2) % length] = 1
            ahead[int(k >= length - 2), r * length + k, r * length + (k + 2) % length] = 1
    sides = np.stack([np.concatenate([back[0] @ f, f, ahead[0] @ f]) for f in flips])
    ends = np.stack([np.concatenate([back[1] @ f, ahead[1] @ f]) for f in flips])
    return flips, sides, ends


def place_of(me, neighbour, rotation, which, patches_here, devices):
    owner = lax.div(neighbour, patches_here)
    within = neighbour - owner * patches_here
    offset = owner - me
    offset = jnp.where(offset < 0, offset + devices, offset)
    core = lax.rem(me, 2)
    to_mate = jnp.where(core == 0, 1, devices - 1)
    block = jnp.where(offset == to_mate, 3, 4)
    block = jnp.where(offset == 2, 2, block)
    block = jnp.where(offset == devices - 2, 1, block)
    block = jnp.where(offset == 0, 0, block)
    slot, code = SIDE_TABLE[which][0]
    for k in range(1, 4):
        slot = jnp.where(rotation == k, SIDE_TABLE[which][k][0], slot)
        code = jnp.where(rotation == k, SIDE_TABLE[which][k][1], code)
    return (block * patches_here + within) * 4 + slot, code


def dot(a, b):
    return jnp.dot(a, b, preferred_element_type=F32)


def column_strip(wide_ref, first, length):
    return jnp.concatenate([wide_ref[pl.ds(first + c, length, stride=length), :] for c in range(2)], axis=0)


def add_columns(wide_ref, first, length, strip):
    for c in range(2):
        at = pl.ds(first + c, length, stride=length)
        wide_ref[at, :] = wide_ref[at, :] + strip[c * length : (c + 1) * length]


def spread(ext_ref, wide, length):
    count = length * length
    size = 2 * length
    column = lax.broadcasted_iota(jnp.int32, (count, 1), 0) & (length - 1)
    back = jnp.where(column >= 2, pltpu.roll(wide, 2, 0), 0.0)
    ahead = jnp.where(column < length - 2, pltpu.roll(wide, count - 2, 0), 0.0)
    for i, part in enumerate((back, wide, ahead)):
        part = part.astype(BF)
        lanes = slice(i * 128, (i + 1) * 128)
        groups = count // (2 * size)
        for g in range(groups):
            at = 2 * size * g
            ext_ref[g, size:, lanes] = part[at : at + size]
            ext_ref[g + 1, 0:size, lanes] = part[at + size : at + 2 * size]


def clear_rows(ext_ref, length):
    size = 2 * length
    empty = jnp.zeros((size, 384), BF)
    ext_ref[0, 0:size, :] = empty
    ext_ref[ext_ref.shape[0] - 1, size:, :] = empty


def pair_taps(rows_of):
    none = jnp.zeros_like(rows_of[0])
    left = rows_of + [none]
    right = [none] + rows_of
    both = [jnp.concatenate([a, b], axis=1) for a, b in zip(left, right)]
    return [jnp.concatenate(both[0:2], axis=0), jnp.concatenate(both[2:4], axis=0)]


def conv_pairs(ext_ref, weights, first, groups, length):
    size = 2 * length
    total = None
    for half in range(2):
        rows = ext_ref[first + half : first + half + groups]
        pixels = jnp.concatenate(
            [rows[:, 0:size].reshape(groups * size, 384), rows[:, size:].reshape(groups * size, 384)], axis=1
        )
        part = dot(pixels, weights[half])
        total = part if total is None else total + part
    return total[:, 0:128].reshape(groups, size, 128), total[:, 128:].reshape(groups, size, 128)


def begin(source, target, sem):
    copy = pltpu.make_async_copy(source, target, sem)
    copy.start()
    return copy


def finish(copies):
    for copy in copies:
        copy.wait()


def pack_kernel(x_ref, out_vm, x_vm, wide_ref, sems, *, length):
    count = length * length
    patches = x_vm.shape[0]
    arriving = [begin(x_ref.at[p], x_vm.at[p], sems.at[p]) for p in range(patches)]
    for p in range(patches):
        arriving[p].wait()
        out_vm[4 * p] = x_vm[p, 0 : 2 * length, :]
        out_vm[4 * p + 1] = x_vm[p, count - 2 * length :, :]
        wide_ref[...] = x_vm[p].astype(F32)
        out_vm[4 * p + 2] = column_strip(wide_ref, 0, length).astype(BF)
        out_vm[4 * p + 3] = column_strip(wide_ref, length - 2, length).astype(BF)


def own_kernel(
    me_ref, nb_ref, rot_ref, cor_ref, x_ref, cot_ref, w_ref, bias_in_ref, flip_ref,
    own_ref, far_ref, near_ref, dw_ref, dx_ref, mid_ref,
    nb_sm, rot_sm, cor_sm, x_vm, cot_vm, w_vm, bias_in_vm, flip_vm,
    strips_vm, near_vm, dw_vm, dx_vm, mid_vm, ext_ref, wide_ref, pool_ref, sems, *, length, devices,
):
    patches = x_vm.shape[0]
    count = length * length
    size = 2 * length
    block = 4 * patches
    sources = [nb_ref, rot_ref, cor_ref, w_ref, bias_in_ref, flip_ref]
    targets = [nb_sm, rot_sm, cor_sm, w_vm, bias_in_vm, flip_vm]
    arriving = [begin(a, b, sems.at[i]) for i, (a, b) in enumerate(zip(sources, targets))]
    used = len(arriving)
    cots = [begin(cot_ref.at[p], cot_vm.at[p], sems.at[used + p]) for p in range(patches)]
    used += patches
    xs = [begin(x_ref.at[p], x_vm.at[p], sems.at[used + p]) for p in range(patches)]
    used += patches
    leaving = []
    me = me_ref[0]
    pool_ref[...] = jnp.zeros_like(pool_ref)
    clear_rows(ext_ref, length)
    along = lax.broadcasted_iota(jnp.int32, (length, 1), 0)
    finish(arriving)
    taps = [jnp.concatenate([w_vm[a * 3 + b] for a, b in SIDE_TAPS[s]], axis=0) for s in range(4)]
    for p in range(patches):
        cots[p].wait()
        mine = slice(size * p, size * (p + 1))
        strips_vm[0, mine, :] = cot_vm[p, 0:size, :]
        strips_vm[1, mine, :] = cot_vm[p, count - size :, :]
        wide_ref[...] = cot_vm[p].astype(F32)
        strips_vm[2, mine, :] = column_strip(wide_ref, 0, length).astype(BF)
        strips_vm[3, mine, :] = column_strip(wide_ref, length - 2, length).astype(BF)
    sent = []
    for s in range(4):
        terms = lax.dot_general(strips_vm[s], taps[s], (((1,), (1,)), ((), ())), preferred_element_type=F32)
        for p in range(patches):
            side, first, last = [], [], []
            for r in range(2):
                rows = slice(size * p + r * length, size * p + (r + 1) * length)
                ahead = pltpu.roll(terms[rows, 0:128], length - 2, 0)
                back = pltpu.roll(terms[rows, 256:384], 2, 0)
                side.append(
                    terms[rows, 128:256]
                    + jnp.where(along < length - 2, ahead, 0.0)
                    + jnp.where(along >= 2, back, 0.0)
                )
                first.append(jnp.where(along >= length - 2, ahead, 0.0))
                last.append(jnp.where(along < 2, back, 0.0))
            sent.append((p, SIDE_DIRECTION[s], side))
            if s < 2:
                sent += [(p, SIDE_ENDS[s][0], first), (p, SIDE_ENDS[s][1], last)]
    placed = []
    for p, j, term in sent:
        where_to, code = place_of(me, nb_sm[p, j], rot_sm[p, j], wanted_side(*DIRECTIONS[j]), patches, devices)
        value = dot(flip_vm[code], jnp.concatenate(term, axis=0).astype(BF))
        placed.append((where_to, value * (cor_sm[p, j] > 0).astype(F32)))
    for where_to, value in placed:
        pool_ref[where_to] = pool_ref[where_to] + value
    near_vm[...] = pool_ref[3 * block :].astype(BF)
    for source, target in (
        (near_vm, near_ref),
        (pool_ref.at[pl.ds(0, block)], own_ref), (pool_ref.at[pl.ds(block, 2 * block)], far_ref),
    ):
        leaving.append(begin(source, target, sems.at[used]))
        used += 1

    total_bias = jnp.zeros((1, 128), F32)
    flipped = pair_taps(
        [jnp.concatenate([w_vm[(2 - a) * 3 + 2 - b].T for b in range(3)], axis=0) for a in range(3)]
    )
    plain = pair_taps([jnp.concatenate([w_vm[a * 3 + b] for b in range(3)], axis=0) for a in range(3)])
    groups = count // (2 * size)
    step = min(groups, STEP)
    for p in range(patches):
        wide = cot_vm[p].astype(F32)
        total_bias = total_bias + jnp.sum(wide, axis=0, keepdims=True)
        spread(ext_ref, wide, length)
        xs[p].wait()
        turned = x_vm[p].T
        windows = [
            ext_ref[0:groups].reshape(count, 384),
            jnp.concatenate([ext_ref[0:groups, size:], ext_ref[1 : groups + 1, 0:size]], axis=1).reshape(count, 384),
            ext_ref[1 : groups + 1].reshape(count, 384),
        ]
        for a in range(3):
            grads = dot(turned, windows[a])
            for b in range(3):
                tap = (2 - a) * 3 + 2 - b
                rows = slice(tap * 128, (tap + 1) * 128)
                part = grads[:, b * 128 : (b + 1) * 128]
                dw_vm[rows, :] = part if p == 0 else dw_vm[rows, :] + part
        for g in range(0, groups, step):
            for i, part in enumerate(conv_pairs(ext_ref, flipped, g, step, length)):
                dx_vm[p, g : g + step, i * size : (i + 1) * size] = part.astype(BF)
        leaving.append(begin(dx_vm.at[p], dx_ref.at[p], sems.at[used]))
        used += 1
    dw_vm[9 * 128 : 10 * 128, :] = jnp.zeros((128, 128), F32)
    dw_vm[9 * 128 : 9 * 128 + 8, :] = jnp.broadcast_to(total_bias, (8, 128))
    for s in range(4):
        at = 10 * 128 + s * patches * size
        dw_vm[at : at + patches * size, :] = strips_vm[s].astype(F32)
    leaving.append(begin(dw_vm, dw_ref, sems.at[used]))
    used += 1
    for p in range(patches):
        spread(ext_ref, x_vm[p].astype(F32), length)
        for g in range(0, groups, step):
            for i, part in enumerate(conv_pairs(ext_ref, plain, g, step, length)):
                mid_vm[p, g : g + step, i * size : (i + 1) * size] = part + bias_in_vm[...]
        leaving.append(begin(mid_vm.at[p], mid_ref.at[p], sems.at[used]))
        used += 1
    finish(leaving)


def halo_kernel(
    me_ref, nb_ref, rot_ref, cor_ref, own_ref, low_ref, high_ref, mate_ref, across_ref, dw_ref,
    side_vm, end_vm, keep_ref, send_ref, halo_ref,
    nb_sm, rot_sm, cor_sm, pool_ref, total_ref, halo_vm, sems, *, length, devices, factor,
):
    block = pool_ref.shape[0] // 5
    patches = block // 4
    sources = [nb_ref, rot_ref, cor_ref]
    targets = [nb_sm, rot_sm, cor_sm]
    arriving = [begin(a, b, sems.at[i]) for i, (a, b) in enumerate(zip(sources, targets))]
    used = len(arriving)
    later = [begin(dw_ref, total_ref, sems.at[used])]
    used += 1
    for i, source in enumerate((own_ref, low_ref, high_ref, mate_ref, across_ref)):
        pool_ref[i * block : (i + 1) * block] = source[...]
    me = me_ref[0]
    size = 2 * length
    finish(arriving)
    for p in range(patches):

        def fetch(j):
            at, code = place_of(me, nb_sm[p, j], rot_sm[p, j], wanted_side(*DIRECTIONS[j]), patches, devices)
            return pool_ref[at], code

        for s in range(4):
            source, code = fetch(SIDE_DIRECTION[s])
            shifted = dot(side_vm[code], source)
            parts = [shifted[0:size], shifted[size : 2 * size], shifted[2 * size :]]
            if s < 2:
                for which, j in ((0, SIDE_ENDS[s][0]), (1, SIDE_ENDS[s][1])):
                    source, code = fetch(j)
                    corner = dot(end_vm[code, which * size : (which + 1) * size, :], source)
                    parts[2 * which] = parts[2 * which] + corner * (cor_sm[p, j] > 0).astype(F32)
            for i in range(3):
                halo_vm[s, p * size : (p + 1) * size, i * 128 : (i + 1) * 128] = parts[i].astype(BF)
    leaving = [begin(halo_vm, halo_ref, sems.at[used])]
    finish(later)
    for s in range(4):
        at = 10 * 128 + s * patches * size
        strips = total_ref[at : at + patches * size, :].astype(BF)
        grads = lax.dot_general(
            halo_vm[s], strips, (((0,), (0,)), ((), ())), preferred_element_type=F32
        )
        for i, (a, b) in enumerate(SIDE_TAPS[s]):
            rows = slice((a * 3 + b) * 128, (a * 3 + b + 1) * 128)
            total_ref[rows, :] = total_ref[rows, :] + grads[i * 128 : (i + 1) * 128]
    taps = 9 * 128
    half = taps // 2
    core = lax.rem(me, 2)
    for target, which in ((send_ref, 1 - core), (keep_ref, core)):
        target[0:half, :] = total_ref[pl.ds(pl.multiple_of(which * half, 64), half), :] * factor
        target[half:, :] = total_ref[taps : taps + target.shape[0] - half, :] * factor
    finish(leaving)


def forward_kernel(mid_ref, w_ref, halo_ref, out_ref, mid_vm, w_vm, halo_vm, out_vm, sems, *, length):
    count = length * length
    size = 2 * length
    patches = mid_vm.shape[0]
    arriving = [begin(w_ref, w_vm, sems.at[0]), begin(halo_ref, halo_vm, sems.at[1])]
    mids = [begin(mid_ref.at[p], mid_vm.at[p], sems.at[2 + p]) for p in range(patches)]
    finish(arriving)
    borders = []
    for s in range(4):
        taps = jnp.concatenate([w_vm[a * 3 + b] for a, b in SIDE_TAPS[s]], axis=0)
        borders.append(dot(halo_vm[s], taps))
    leaving = []
    for p in range(patches):
        mids[p].wait()
        mine = slice(p * size, (p + 1) * size)
        wide_ref = mid_vm.at[p]
        wide_ref[0:size, :] = wide_ref[0:size, :] + borders[0][mine]
        wide_ref[count - size :, :] = wide_ref[count - size :, :] + borders[1][mine]
        add_columns(wide_ref, 0, length, borders[2][mine])
        add_columns(wide_ref, length - 2, length, borders[3][mine])
        out_vm[p] = wide_ref[...].astype(BF)
        leaving.append(begin(out_vm.at[p], out_ref.at[p], sems.at[2 + patches + p]))
    finish(leaving)


def join_kernel(
    dx_ref, own_ref, near_ref, low_ref, high_ref, out_ref,
    dx_vm, own_vm, out_vm, wide_ref, sems, *, length,
):
    count = length * length
    size = 2 * length
    patches = dx_vm.shape[0]
    arriving = [begin(own_ref, own_vm, sems.at[0])]
    used = len(arriving)
    dxs = [begin(dx_ref.at[p], dx_vm.at[p], sems.at[used + p]) for p in range(patches)]
    used += patches
    finish(arriving)
    leaving = []
    for p in range(patches):
        dxs[p].wait()
        wide_ref[...] = dx_vm[p].astype(F32)
        strips = []
        for s in range(4):
            i = 4 * p + s
            strips.append(own_vm[i] + near_ref[i].astype(F32) + low_ref[i].astype(F32) + high_ref[i].astype(F32))
        wide_ref[0:size, :] = wide_ref[0:size, :] + strips[0]
        wide_ref[count - size :, :] = wide_ref[count - size :, :] + strips[1]
        add_columns(wide_ref, 0, length, strips[2])
        add_columns(wide_ref, length - 2, length, strips[3])
        out_vm[p] = wide_ref[...].astype(BF)
        leaving.append(begin(out_vm.at[p], out_ref.at[p], sems.at[used]))
        used += 1
    finish(leaving)


def half_kernel(me_ref, half_ref, *refs, mates):
    grad_ref, sem = refs[1 if mates else 0], refs[-1]
    half = grad_ref.shape[0] // 2
    core = lax.rem(me_ref[0], 2)
    at = (1 - core) * half if mates else core * half
    copy = begin(half_ref.at[pl.ds(0, half)], grad_ref.at[pl.ds(pl.multiple_of(at, 64), half)], sem.at[0])
    if not mates:
        bias_ref = refs[1]
        bias_ref[...] = half_ref[half : half + 1, :]
    copy.wait()


def call(kernel, name, operands, outs, scratch, copies, small=(), room=4, aliases=None):
    spaces = {"s": pltpu.SMEM, "h": pltpu.HBM, "a": pl.ANY, "v": pltpu.VMEM}
    out_specs = [pl.BlockSpec(memory_space=pltpu.VMEM if i in small else pl.ANY) for i in range(len(outs))]
    return pl.pallas_call(
        kernel,
        name=name,
        out_shape=list(outs),
        input_output_aliases=aliases or {},
        in_specs=[pl.BlockSpec(memory_space=spaces[o]) for o in operands],
        out_specs=out_specs,
        scratch_shapes=list(scratch) + [pltpu.SemaphoreType.DMA((copies,))],
        compiler_params=pltpu.CompilerParams(vmem_limit_bytes=(64 - room) * 1024 * 1024),
        cost_estimate=pl.CostEstimate(flops=0, bytes_accessed=0, transcendentals=0),
    )


def shifted(value, steps):
    count = lax.axis_size("patch")
    return lax.ppermute(value, "patch", [(d, (d + steps) % count) for d in range(count)])


def swapped(value, mask):
    return lax.ppermute(value, "patch", [(d, d ^ mask) for d in range(lax.axis_size("patch"))])


def part_of(value, index, size):
    return lax.dynamic_slice_in_dim(value, index * size, size)


def summed(keep, send, me, devices, between, last):
    mine = keep + swapped(send, 1)
    quarter = mine.shape[0] // 4
    at = (me // 2) % 4
    arrived = [swapped(part_of(mine, at ^ k, quarter).astype(BF), 2 * k) for k in (3, 2, 1)]
    mine = part_of(mine, at, quarter)
    for a in arrived:
        mine = mine + a.astype(F32)
    step = 8
    while step < devices:
        sent = mine.astype(BF)
        arrived = [swapped(sent, k * step) for k in ((3, 2, 1) if 2 * step < devices else (1,))][::-1]
        if 4 * step >= devices:
            arrived = between(arrived)
        mine = sent.astype(F32) + arrived[0].astype(F32)
        if len(arrived) > 1:
            mine = mine + (arrived[1].astype(F32) + arrived[2].astype(F32))
        step *= 4
    pieces = jnp.stack([mine] + [swapped(mine, 2 * k) for k in range(1, 4)])
    whole = jnp.concatenate([lax.dynamic_index_in_dim(pieces, at ^ k, 0, False) for k in range(4)])
    whole = last(whole)
    return whole, swapped(whole, 1)


def own_pixels(tables, x, cot, w, bias, flips, devices):
    patches, count, chans = x.shape
    length = math.isqrt(count)
    size = 2 * length
    block = 4 * patches
    rows = 10 * chans
    grouped = (patches, count // (2 * size), 2 * size, chans)
    shape = jax.ShapeDtypeStruct
    scratch = pltpu.VMEM
    table_scratch = [pltpu.SMEM(tables[1].shape, jnp.int32)] * 3
    return call(
        functools.partial(own_kernel, length=length, devices=devices), "own_pixels", "shhhhhhhh",
        [
            shape((block, size, chans), F32),
            shape((2 * block, size, chans), F32),
            shape((2 * block, size, chans), BF),
            shape((rows + block * size, chans), F32),
            shape(grouped, BF),
            shape(grouped, F32),
        ],
        table_scratch
        + [
            scratch(x.shape, BF),
            scratch(x.shape, BF),
            scratch(w.shape, BF),
            scratch((1, chans), F32),
            scratch(flips.shape, BF),
            scratch((4, patches * size, chans), BF),
            scratch((2 * block, size, chans), BF),
            scratch((rows + block * size, chans), F32),
            scratch(grouped, BF),
            scratch(grouped, F32),
            scratch((count // (2 * size) + 1, 2 * size, 3 * chans), BF),
            scratch((count, chans), F32),
            scratch((5 * block, size, chans), F32),
        ],
        6 + 4 * patches + 4,
    )(*tables, x, cot, w, bias, flips)


def body(inputs, cotangent, weights, bias_vector, neighbours, rotations, corners):
    patches, length, _, chans = inputs.shape
    devices = lax.axis_size("patch")
    count = length * length
    size = 2 * length
    block = 4 * patches
    rows = 10 * chans
    me = lax.axis_index("patch")
    me_arr = me.reshape(1).astype(jnp.int32)
    core = me % 2
    x = inputs.reshape(patches, count, chans)
    cot = cotangent.reshape(patches, count, chans)
    w = weights.reshape(9, chans, chans)
    flips, sides, ends = (jnp.asarray(t, BF) for t in flip_tables(length))
    shape = jax.ShapeDtypeStruct
    scratch = pltpu.VMEM
    tables = (me_arr, neighbours, rotations, corners)
    table_scratch = [pltpu.SMEM(neighbours.shape, jnp.int32)] * 3

    (edges,) = call(
        functools.partial(pack_kernel, length=length), "pack_edges", "h", [shape((block, size, chans), BF)],
        [scratch(x.shape, BF), scratch((count, chans), F32)], patches, small=(0,), room=ROOM,
    )(x)
    from_low = shifted(edges, 2)
    from_high = shifted(edges, -2)
    from_mate = swapped(edges, 1)

    own, far, near, dw, dx, mid = own_pixels(tables, x, cot, w, bias_vector.reshape(1, chans), flips, devices)
    dx, mid = dx.reshape(x.shape), mid.reshape(x.shape)
    near_in = swapped(near, 1)

    from_low, from_high, dw = lax.optimization_barrier((from_low, from_high, dw))
    from_across = swapped(jnp.where(core == 0, from_high, from_low), 1)

    cross_terms = near_in[block:].astype(F32)
    to_low = (far[:block] + jnp.where(core == 1, cross_terms, 0.0)).astype(BF)
    to_high = (far[block:] + jnp.where(core == 0, cross_terms, 0.0)).astype(BF)

    factor = 1.0 / (length * math.sqrt(patches * devices))
    keep, send, halo = call(
        functools.partial(halo_kernel, length=length, devices=devices, factor=factor), "halo_kernel_grad",
        "shhhvvvvvavv",
        [
            shape((rows // 2, chans), F32),
            shape((rows // 2, chans), F32),
            shape((4, patches * size, 3 * chans), BF),
        ],
        table_scratch
        + [
            scratch((5 * block, size, chans), BF),
            scratch(dw.shape, F32),
            scratch((4, patches * size, 3 * chans), BF),
        ],
        5, small=(0, 1), room=ROOM,
    )(*tables, edges, from_low, from_high, from_mate, from_across, dw, sides, ends)

    (outputs,) = call(
        functools.partial(forward_kernel, length=length), "add_halo_outputs", "aha", [shape(x.shape, BF)],
        [scratch(x.shape, F32), scratch(w.shape, BF), scratch(halo.shape, BF), scratch(x.shape, BF)], 2 + 2 * patches, room=ROOM,
    )(mid, w, halo)

    terms_high = shifted(to_low, -2)
    terms_low = shifted(to_high, 2)
    results = {}

    def between(value):
        value, results["low"] = lax.optimization_barrier((value, terms_low))
        results["high"] = terms_high
        return value

    def last(value):
        (input_grad,) = call(
            functools.partial(join_kernel, length=length), "join_input_grad", "aavvv", [shape(x.shape, BF)],
            [
                scratch(x.shape, BF),
                scratch((block, size, chans), F32),
                scratch(x.shape, BF),
                scratch((count, chans), F32),
            ],
            1 + 2 * patches, room=ROOM,
        )(dx, own, near_in, results["low"], results["high"])
        value, results["in"], results["out"] = lax.optimization_barrier((value, input_grad, outputs))
        return value

    mine, other = summed(keep, send, me, devices, between, last)
    grad_shapes = [shape((9 * chans, chans), F32), shape((1, chans), F32)]
    weight_grad, bias_grad = call(
        functools.partial(half_kernel, mates=False), "place_own_half", "sv", grad_shapes, [], 1, small=(1,), room=ROOM,
    )(me_arr, mine)
    (weight_grad,) = call(
        functools.partial(half_kernel, mates=True), "place_mates_half", "sva", grad_shapes[:1], [], 1, room=ROOM,
        aliases={2: 0},
    )(me_arr, other, weight_grad)
    return (
        results["out"].reshape(inputs.shape),
        results["in"].reshape(inputs.shape),
        weight_grad.reshape(weights.shape),
        bias_grad.reshape(bias_vector.shape),
    )


def solution(mesh):
    in_specs = (
        P("patch", None, None, None),
        P("patch", None, None, None),
        P(),
        P(),
        P("patch", None),
        P("patch", None),
        P("patch", None),
    )
    out_specs = (P("patch", None, None, None), P("patch", None, None, None), P(), P())
    return jax.shard_map(body, mesh=mesh, in_specs=in_specs, out_specs=out_specs, check_vma=False)
```
